1024 devices in a mesh: comp: 32 (over z, x_lo), tile: 32 (over x_hi, y, core).
Axes of the slice: x: 8 (x_hi: 2, x_lo: 4; x = x_hi * 4 + x_lo), y: 8, z: 8, core: 2. Of those that a mesh axis runs over, the one named last changes fastest.
Arguments:
- tracers: float32 [2, 72, 256, 4096], P(None, None, 'tile', 'comp'), may hold values from -8 to 8
- surface_fields: float32 [4, 256, 4096], P(None, 'tile', 'comp'), may hold values from -6 to 6
- lateral_rate: bfloat16 [256, 4096], P('tile', 'comp'), may hold values from 0.0099487305 to 0.19921875
- vertical_rate: bfloat16 [71, 256, 4096], P(None, 'tile', 'comp'), may hold values from 0.0029907227 to 0.25
- coupling_gain: float32 [32, 2, 4], P('comp'), may hold values from -4 to 4
- send_slots: int32 [32, 32, 32, 2], P('comp', None, 'tile'), may hold values from -1 to 7, as said below
- recv_slots: int32 [32, 32, 32, 2], P('comp', None, 'tile'), may hold values from -1 to 7, as said below
- remap_weights: bfloat16 [32, 32, 32, 2, 128, 128], P('comp', None, 'tile'), may hold values from -0.5 to 0.5
Outputs:
- tracers_next: float32 [2, 72, 256, 4096], P(None, None, 'tile', 'comp')
The draws below stay inside these ranges and needn't reach their ends.
Inputs may be any that keep to these rules, and one draw needn't show every extreme that they name: `send_slots`: -1 marks an empty slot, else a block of the sender. Slots are live only between an atmosphere row and an ocean row, each such pair of devices having 1 to 2 live slots, live ones first; most such pairs fill all 2, in every tile and from every receiver's view too. recv_slots[q, r, t, s] is live exactly where send_slots[r, q, t, s] is, and then names a block of the receiver; -1 elsewhere.
All inputs are finite; a program needn't handle non-finite values.
Results may differ from the reference program's by a relative error of at most 0.00045.
Values sent between devices are 32-bit elements; how exact they have to be, the bound alone decides.
A program may use at most 32 MiB of HBM per device.

```python
import math
import jax
import jax.numpy as jnp
from jax import lax

VARS = 2
LEV = 72
OLEV = 60
FIELDS = 4
STEPS = 2
SLOT = 2
CY = 128
CX = 8
ROWS = 32
TILES = 32
ATM_ROWS = 24
NX = 256
NY = 4096


def coupling_lists(key):
    key_count, key_send, key_recv = jax.random.split(key, 3)
    shape = (ROWS, ROWS, TILES)
    counts = jax.random.randint(key_count, shape, 1, SLOT + 1)
    rows_index = jnp.arange(ROWS, dtype=jnp.int32)
    tiles_index = jnp.arange(TILES, dtype=jnp.int32)
    atmos = rows_index < 3 * ROWS // 4
    crossing = atmos[:, None] != atmos[None, :]
    filled = (rows_index[:, None, None] + rows_index[None, :, None] + tiles_index[None, None, :]) % 3 != 0
    counts = jnp.where(filled, SLOT, counts)
    counts = jnp.where(crossing[:, :, None], counts, 0)
    live = jnp.arange(SLOT, dtype=jnp.int32) < counts[..., None]
    full_shape = (ROWS, ROWS, TILES, SLOT)
    sender = jnp.where(live, jax.random.randint(key_send, full_shape, 0, CX), -1)
    receiver = jnp.where(live, jax.random.randint(key_recv, full_shape, 0, CX), -1)
    return (sender.astype(jnp.int32), receiver.astype(jnp.int32))


def draw_send_slots(key, part):
    sender, receiver = coupling_lists(key)
    return sender


def draw_recv_slots(key, part):
    sender, receiver = coupling_lists(key)
    return jnp.transpose(receiver, (1, 0, 2, 3))


def shard_levels(rng, extent, cuts, low, largest):
    loudness = 1.0
    for dim, blocks in cuts:
        heights = jax.random.uniform(jax.random.fold_in(jax.random.fold_in(rng, 6), dim), (blocks,), jnp.float32, low / len(cuts), largest / len(cuts))
        loudness = loudness * jnp.repeat(jnp.exp(heights), extent[dim] // blocks).reshape((-1,) + (1,) * (len(extent) - 1 - dim))
    return loudness


def bell_draw(stream_key, dims, spread, most, shards=(), kind=jnp.bfloat16):
    values = spread * jax.random.normal(stream_key, dims, jnp.float32)
    if shards:
        values = values * shard_levels(stream_key, dims, shards, -0.22, 0.18)
    return jnp.clip(values, -most, most).astype(kind)


def setup_inputs(seed: int = 0) -> dict:
    key_of = jax.random.split(jax.random.key(seed), 9)
    return {
        "tracers": jnp.clip(jax.random.uniform(key_of[0], (VARS, LEV, NX, NY), jnp.float32, -8.0, 8.0) * shard_levels(key_of[0], (VARS, LEV, NX, NY), ((2, 32), (3, 32)), -0.4, 0.0), -8.0, 8.0),
        "surface_fields": bell_draw(key_of[1], (FIELDS, NX, NY), 1.0, 6.0, ((1, 32), (2, 32)), jnp.float32),
        "lateral_rate": jnp.clip(0.0099487305 + 0.18927002 * jax.random.uniform(key_of[2], (NX, NY), jnp.float32) ** shard_levels(key_of[2], (NX, NY), ((0, 32), (1, 32)), -0.2, 0.2), 0.0099487305, 0.19921875).astype(jnp.bfloat16),
        "vertical_rate": jnp.clip(jnp.exp(math.log(0.25) - 4.4259459 * jax.random.uniform(key_of[3], (LEV - 1, NX, NY), jnp.float32) ** shard_levels(key_of[3], (LEV - 1, NX, NY), ((1, 32), (2, 32)), -0.2, 0.2)), 0.0029907227, 0.25).astype(jnp.bfloat16),
        "coupling_gain": bell_draw(key_of[4], (ROWS, VARS, FIELDS), 1.0, 4.0, ((0, 32),), jnp.float32),
        "send_slots": draw_send_slots(jax.random.fold_in(key_of[8], 71), 0),
        "recv_slots": draw_recv_slots(jax.random.fold_in(key_of[8], 71), 0),
        "remap_weights": bell_draw(key_of[7], (ROWS, ROWS, TILES, SLOT, CY, CY), CY ** -0.5, 0.5, ((0, 32), (2, 32))),
    }


def advance(extended, lateral, vertical, forcing, active):
    centre = extended[:, :, 1:-1, 1:-1]
    laplace = (extended[:, :, 2:, 1:-1] + extended[:, :, :-2, 1:-1]
               + extended[:, :, 1:-1, 2:] + extended[:, :, 1:-1, :-2] - 4.0 * centre)
    coupled = vertical * active[1:].astype(jnp.float32)
    flux_down = coupled * (centre[:, 1:] - centre[:, :-1])
    zero_level = jnp.zeros_like(flux_down[:, :1])
    mixing = jnp.concatenate([flux_down, zero_level], 1) - jnp.concatenate([zero_level, flux_down], 1)
    updated = centre + lateral * laplace + mixing
    updated = updated.at[:, 0].add(forcing)
    return jnp.where(active, updated, centre)


def region_step(field, lateral, vertical, forcing, active):
    extended = jnp.pad(field, ((0, 0), (0, 0), (0, 0), (1, 1)), mode="edge")
    extended = jnp.pad(extended, ((0, 0), (0, 0), (1, 1), (0, 0)), mode="wrap")
    return advance(extended, lateral, vertical, forcing, active)


def reference(tracers, surface_fields, lateral_rate, vertical_rate, coupling_gain, send_slots, recv_slots, remap_weights):
    highest = lax.Precision.HIGHEST
    blocks = surface_fields.reshape(FIELDS, TILES, CX, ROWS, CY)
    blocks = jnp.transpose(blocks, (3, 1, 2, 0, 4))
    columns = jnp.arange(CX, dtype=jnp.int32)

    def one_row(target):
        chosen = jnp.take(send_slots, target, axis=1)
        picker = (chosen[..., None] == columns).astype(jnp.float32)
        picked = jnp.einsum("rtsx,rtxfj->rtsfj", picker, blocks, precision=highest)
        weights = jnp.take(remap_weights, target, axis=0).astype(jnp.float32)
        contrib = jnp.einsum("rtsfi,rtsij->rtsfj", picked, weights, precision=highest)
        landing = (jnp.take(recv_slots, target, axis=0)[..., None] == columns).astype(jnp.float32)
        return jnp.einsum("rtsx,rtsfj->tfxj", landing, contrib, precision=highest)

    remapped = lax.map(one_row, jnp.arange(ROWS, dtype=jnp.int32))
    remapped = jnp.transpose(remapped, (2, 1, 3, 0, 4)).reshape(FIELDS, NX, NY)
    gain_cells = jnp.repeat(coupling_gain, CY, axis=0)
    forcing = jnp.einsum("yvf,fxy->vxy", gain_cells, remapped, precision=highest)

    split = ATM_ROWS * CY
    lateral = lateral_rate.astype(jnp.float32)
    vertical = vertical_rate.astype(jnp.float32)
    levels = jnp.arange(LEV, dtype=jnp.int32)
    atmos_active = jnp.ones((LEV, 1, 1), dtype=bool)
    ocean_active = (levels < OLEV)[:, None, None]
    current = tracers
    for repeat in range(STEPS):
        upper = region_step(current[..., :split], lateral[:, :split], vertical[..., :split],
                            forcing[..., :split], atmos_active)
        lower = region_step(current[..., split:], lateral[:, split:], vertical[..., split:],
                            forcing[..., split:], ocean_active)
        current = jnp.concatenate([upper, lower], -1)
    return current
```

```python
import functools

import jax
import jax.numpy as jnp
from jax import lax
from jax.experimental import pallas as pl
from jax.experimental.pallas import tpu as pltpu
from jax.sharding import PartitionSpec as P

OLEV = 60
CHUNK = 24
MESH = pl.DeviceIdType.MESH


def tile_of(index):
    return pl.ds(pl.multiple_of(index * 8, 8), 8)


def kernel(
    levels,
    tracers,
    fields,
    lateral,
    vertical,
    gain,
    send_slots,
    recv_slots,
    weights,
    out,
    first,
    second,
    lat,
    ver,
    rate,
    surf,
    blocks,
    outgoing,
    incoming,
    spread,
    wts,
    forcing,
    gains,
    sends,
    recvs,
    x_out,
    x_in,
    y_out,
    y_in,
    x0_out,
    x0_in,
    y0_out,
    y0_in,
    load_sem,
    remap_send,
    remap_recv,
    x_send,
    x_recv,
    y_send,
    y_recv,
    x0_send,
    x0_recv,
    y0_send,
    y0_recv,
):
    rows = lax.axis_size("comp")
    tiles = lax.axis_size("tile")
    atmos = 3 * rows // 4
    ocean = rows - atmos
    row = lax.axis_index("comp")
    tile = lax.axis_index("tile")
    left = lax.rem(tile + tiles - 1, tiles)
    right = lax.rem(tile + 1, tiles)
    is_ocean = row >= atmos
    is_atmos = row < atmos
    has_lower = jnp.logical_and(row != 0, row != atmos)
    has_upper = jnp.logical_and(row != atmos - 1, row != rows - 1)
    no_lower = jnp.logical_or(row == 0, row == atmos)
    no_upper = jnp.logical_or(row == atmos - 1, row == rows - 1)
    live_levels = jnp.where(is_ocean, OLEV, levels)
    chunks = levels // CHUNK
    lane = lax.broadcasted_iota(jnp.int32, (8, 128), 1)
    sub = lax.broadcasted_iota(jnp.int32, (8, 128), 0)

    loads = [
        pltpu.make_async_copy(source, target, load_sem.at[place])
        for place, (source, target) in enumerate(
            [
                (fields, surf),
                (send_slots, sends),
                (tracers, first),
                (vertical, ver),
                (lateral, lat),
                (recv_slots, recvs),
                (gain, gains),
            ]
        )
    ]
    get_fields, get_sends, get_tracers, get_vertical, get_lateral, get_recvs, get_gain = loads
    for load in loads:
        load.start()

    def get_weights(base, count):
        return pltpu.make_async_copy(
            weights.at[pl.ds(base, count)], wts.at[pl.ds(0, count)], load_sem.at[7]
        )

    @pl.when(is_ocean)
    def _():
        get_weights(0, atmos).start()

    @pl.when(is_atmos)
    def _():
        get_weights(atmos, ocean).start()

    barrier = pltpu.get_barrier_semaphore()

    def greet(to_row, to_tile):
        pl.semaphore_signal(barrier, inc=1, device_id=(to_row, to_tile), device_id_type=MESH)

    greet(row, left)
    greet(row, right)

    @pl.when(has_lower)
    def _():
        greet(row - 1, tile)

    @pl.when(has_upper)
    def _():
        greet(row + 1, tile)

    @pl.when(is_ocean)
    def _():
        for partner in range(atmos):
            greet(partner, tile)

    @pl.when(is_atmos)
    def _():
        for partner in range(atmos, rows):
            greet(partner, tile)

    get_fields.wait()
    get_sends.wait()
    for block in range(8):
        picked = surf[pl.ds(block, 4, stride=8), :]
        blocks[block, 0:4, :] = picked
        blocks[block, 4:8, :] = picked
    blocks[8] = jnp.zeros((8, 128), jnp.float32)

    def fill(base, count):
        def one(place, carry):
            slot0 = sends[0, base + place]
            slot1 = sends[1, base + place]
            slot0 = jnp.where(slot0 < 0, 8, slot0)
            slot1 = jnp.where(slot1 < 0, 8, slot1)
            outgoing[place] = jnp.where(sub < 4, blocks[slot0], blocks[slot1])
            return carry

        lax.fori_loop(0, count, one, 0, unroll=4)

    @pl.when(is_ocean)
    def _():
        fill(0, atmos)

    @pl.when(is_atmos)
    def _():
        fill(atmos, ocean)

    def pack_x(step, chunk, source):
        for var in range(2):
            start = (var * levels + chunk * CHUNK) * 8
            here = pl.ds(pl.multiple_of(chunk * CHUNK, 8), CHUNK)
            x_out[step, 1, var, here, :] = source[pl.ds(start, CHUNK, stride=8), :]
            x_out[step, 0, var, here, :] = source[pl.ds(start + 7, CHUNK, stride=8), :]

    def add_lanes(low, high, value, entry):
        turned = pltpu.roll(value, 2 * entry, 1) if entry else value
        low = jnp.where(lane == 2 * entry, turned, low)
        high = jnp.where(lane == (2 * entry + 127) % 128, turned, high)
        return low, high

    def put_y(target, wall, low, high):
        target[1] = low
        target[0] = high

        @pl.when(no_lower)
        def _():
            wall[0] = pltpu.roll(low, 127, 1)

        @pl.when(no_upper)
        def _():
            wall[1] = pltpu.roll(high, 1, 1)

    def copy_x(step, chunk, side):
        here = pl.ds(pl.multiple_of(chunk * CHUNK, 8), CHUNK)
        return pltpu.make_async_remote_copy(
            src_ref=x_out.at[step, side, :, here, :],
            dst_ref=x_in.at[step, side, :, here, :],
            send_sem=x_send.at[step, side, chunk],
            recv_sem=x_recv.at[step, side, chunk],
            device_id=(row, left if side else right),
            device_id_type=MESH,
        )

    def copy_y(step, chunk, side):
        return pltpu.make_async_remote_copy(
            src_ref=y_out.at[step, chunk, side],
            dst_ref=y_in.at[step, chunk, side],
            send_sem=y_send.at[step, side, chunk],
            recv_sem=y_recv.at[step, side, chunk],
            device_id=(row - 1 if side else row + 1, tile),
            device_id_type=MESH,
        )

    def copy_x0(side):
        return pltpu.make_async_remote_copy(
            src_ref=x0_out.at[side],
            dst_ref=x0_in.at[side],
            send_sem=x0_send.at[side],
            recv_sem=x0_recv.at[side],
            device_id=(row, left if side else right),
            device_id_type=MESH,
        )

    def copy_y0(side):
        return pltpu.make_async_remote_copy(
            src_ref=y0_out.at[side],
            dst_ref=y0_in.at[side],
            send_sem=y0_send.at[side],
            recv_sem=y0_recv.at[side],
            device_id=(row - 1 if side else row + 1, tile),
            device_id_type=MESH,
        )

    def start_edges(step, chunk):
        copy_x(step, chunk, 0).start()
        copy_x(step, chunk, 1).start()

        @pl.when(has_lower)
        def _():
            copy_y(step, chunk, 1).start()

        @pl.when(has_upper)
        def _():
            copy_y(step, chunk, 0).start()

    def await_edges(step, chunk):
        copy_x(step, chunk, 0).wait_recv()
        copy_x(step, chunk, 1).wait_recv()

        @pl.when(has_lower)
        def _():
            copy_y(step, chunk, 0).wait_recv()

        @pl.when(has_upper)
        def _():
            copy_y(step, chunk, 1).wait_recv()

    def end_edges(step, chunk):
        copy_x(step, chunk, 0).wait_send()
        copy_x(step, chunk, 1).wait_send()

        @pl.when(has_lower)
        def _():
            copy_y(step, chunk, 1).wait_send()

        @pl.when(has_upper)
        def _():
            copy_y(step, chunk, 0).wait_send()

    get_tracers.wait()

    def pack_first(turn, carry):
        chunk = chunks - 1 - turn
        pack_x(0, chunk, first)
        low = high = jnp.zeros((8, 128), jnp.float32)
        for level in range(CHUNK):
            for var in range(2):
                value = first[tile_of(var * levels + chunk * CHUNK + level), :]
                low, high = add_lanes(low, high, value, 2 * level + var)
        put_y(y_out.at[0, chunk], y_in.at[0, chunk], low, high)
        return carry

    lax.fori_loop(0, chunks, pack_first, 0)

    others = jnp.where(is_ocean, atmos, ocean)
    beside = has_lower.astype(jnp.int32) + has_upper.astype(jnp.int32)
    pl.semaphore_wait(barrier, others + beside + 2)

    def copy_block(base, count, own_base, place):
        return pltpu.make_async_remote_copy(
            src_ref=outgoing.at[place],
            dst_ref=incoming.at[row - own_base],
            send_sem=remap_send,
            recv_sem=remap_recv,
            device_id=(base + place, tile),
            device_id_type=MESH,
        )

    def send_blocks(base, count, own_base):
        def one(turn, carry):
            place = lax.rem(turn + row + tile, count)
            copy_block(base, count, own_base, place).start()
            return carry

        lax.fori_loop(0, count, one, 0)

    @pl.when(is_ocean)
    def _():
        send_blocks(0, atmos, atmos)

    @pl.when(is_atmos)
    def _():
        send_blocks(atmos, ocean, 0)

    def send_first(turn, carry):
        start_edges(0, chunks - 1 - turn)
        return carry

    lax.fori_loop(0, chunks, send_first, 0)

    get_vertical.wait()
    get_lateral.wait()
    rate[0] = jnp.zeros((8, 128), jnp.float32)
    rate[levels] = jnp.zeros((8, 128), jnp.float32)

    def one_rate(level, carry):
        value = ver[level].astype(jnp.float32)
        rate[level + 1] = jnp.where(level + 1 < live_levels, value, 0.0)
        return carry

    lax.fori_loop(0, levels - 1, one_rate, 0, unroll=8)

    def advance(step, chunk, source, target, merged, edges):
        lateral_here = lat[...].astype(jnp.float32)
        base = chunk * CHUNK
        previous = [None, None]
        centre = [None, None]
        low = high = jnp.zeros((8, 128), jnp.float32)
        for var in range(2):
            centre[var] = source[tile_of(var * levels + base), :]
            above = source[tile_of(var * levels + jnp.maximum(base - 1, 0)), :]
            previous[var] = rate[base] * (centre[var] - above)
        for level in range(CHUNK):
            here = base + level
            mixing = rate[here + 1]
            spreading = jnp.where(here < live_levels, lateral_here, 0.0)
            for var in range(2):
                entry = 2 * level + var
                after = jnp.minimum(here + 1, levels - 1) if level == CHUNK - 1 else here + 1
                value = centre[var]
                below = source[tile_of(var * levels + after), :]
                x_low = jnp.broadcast_to(x_in[step, 0, var, pl.ds(here, 1), :], (8, 128))
                x_high = jnp.broadcast_to(x_in[step, 1, var, pl.ds(here, 1), :], (8, 128))
                ends = pltpu.roll(merged, 127 - 2 * entry, 1)
                sides = (
                    jnp.where(sub == 0, x_low, pltpu.roll(value, 1, 0))
                    + jnp.where(sub == 7, x_high, pltpu.roll(value, 7, 0))
                ) + (
                    jnp.where(lane == 0, ends, pltpu.roll(value, 1, 1))
                    + jnp.where(lane == 127, ends, pltpu.roll(value, 127, 1))
                )
                down = mixing * (below - value)
                result = value + spreading * (sides - 4.0 * value) + (down - previous[var])
                target[tile_of(var * levels + here), :] = result
                if edges:
                    low, high = add_lanes(low, high, result, entry)
                centre[var] = below
                previous[var] = down
        return low, high

    def merge(low, high):
        return jnp.where(lane % 2 == 1, pltpu.roll(low, 2, 1), high)

    def step_one(turn, carry):
        chunk = chunks - 1 - turn
        await_edges(0, chunk)
        merged = merge(y_in[0, chunk, 0], y_in[0, chunk, 1])
        low, high = advance(0, chunk, first, second, merged, True)
        pack_x(1, chunk, second)
        put_y(y_out.at[1, chunk], y_in.at[1, chunk], low, high)
        start_edges(1, chunk)
        return carry

    lax.fori_loop(0, chunks, step_one, 0)

    get_recvs.wait()
    get_gain.wait()

    def remap(base, count):
        pltpu.make_async_copy(
            incoming.at[pl.ds(0, count)], incoming.at[pl.ds(0, count)], remap_recv
        ).wait()

        def one(place, carry):
            for slot in range(2):
                lands = sub == recvs[slot, base + place]
                column = pl.ds(pl.multiple_of((place * 2 + slot) * 128, 128), 128)
                for pair in range(2):
                    value = jnp.concatenate(
                        [
                            jnp.where(
                                lands,
                                jnp.broadcast_to(
                                    incoming[place, slot * 4 + field : slot * 4 + field + 1, :],
                                    (8, 128),
                                ),
                                0.0,
                            )
                            for field in (2 * pair, 2 * pair + 1)
                        ],
                        axis=0,
                    )
                    coarse = value.astype(jnp.bfloat16)
                    fine = (value - coarse.astype(jnp.float32)).astype(jnp.bfloat16)
                    spread[16 * pair : 16 * pair + 16, column] = coarse
                    spread[32 + 16 * pair : 48 + 16 * pair, column] = fine
            return carry

        lax.fori_loop(0, count, one, 0, unroll=2)
        get_weights(base, count).wait()
        total = jnp.dot(
            spread[:, : count * 256],
            wts[:count].reshape(count * 256, 128),
            preferred_element_type=jnp.float32,
        )
        remapped = total[:32] + total[32:]
        low = high = jnp.zeros((8, 128), jnp.float32)
        values = []
        for var in range(2):
            force = gains[var, 0] * remapped[:8]
            for field in range(1, 4):
                force = force + gains[var, field] * remapped[8 * field : 8 * field + 8]
            forcing[var] = force
            value = second[tile_of(var * levels), :] + force
            second[tile_of(var * levels), :] = value
            low, high = add_lanes(low, high, value, var)
            values.append(value)
        x0_out[1] = jnp.where(sub == 0, values[0][0:1, :], values[1][0:1, :])
        x0_out[0] = jnp.where(sub == 0, values[0][7:8, :], values[1][7:8, :])
        put_y(y0_out, y0_in, low, high)

    @pl.when(is_ocean)
    def _():
        remap(0, atmos)

    @pl.when(is_atmos)
    def _():
        remap(atmos, ocean)

    copy_x0(0).start()
    copy_x0(1).start()

    @pl.when(has_lower)
    def _():
        copy_y0(1).start()

    @pl.when(has_upper)
    def _():
        copy_y0(0).start()

    def step_two(turn, carry):
        chunk = chunks - 1 - turn
        await_edges(1, chunk)
        merged = merge(y_in[1, chunk, 0], y_in[1, chunk, 1])
        advance(1, chunk, second, out, merged, False)
        return carry

    lax.fori_loop(0, chunks - 1, step_two, 0)

    await_edges(1, 0)
    copy_x0(0).wait_recv()
    copy_x0(1).wait_recv()

    @pl.when(has_lower)
    def _():
        copy_y0(0).wait_recv()

    @pl.when(has_upper)
    def _():
        copy_y0(1).wait_recv()

    for side in range(2):
        for var in range(2):
            x_in[1, side, var, 0:1, :] = x0_in[side, var : var + 1, :]
    merged = jnp.where(
        lane < 4, merge(y0_in[0], y0_in[1]), merge(y_in[1, 0, 0], y_in[1, 0, 1])
    )
    advance(1, 0, second, out, merged, False)
    for var in range(2):
        out[tile_of(var * levels), :] += forcing[var]

    for step in range(2):

        def end(chunk, carry):
            end_edges(step, chunk)
            return carry

        lax.fori_loop(0, chunks, end, 0)
    copy_x0(0).wait_send()
    copy_x0(1).wait_send()

    @pl.when(has_lower)
    def _():
        copy_y0(1).wait_send()

    @pl.when(has_upper)
    def _():
        copy_y0(0).wait_send()

    @pl.when(is_ocean)
    def _():
        pltpu.make_async_copy(
            outgoing.at[pl.ds(0, atmos)], outgoing.at[pl.ds(0, atmos)], remap_send
        ).wait()

    @pl.when(is_atmos)
    def _():
        pltpu.make_async_copy(
            outgoing.at[pl.ds(0, ocean)], outgoing.at[pl.ds(0, ocean)], remap_send
        ).wait()


def per_device(
    tracers,
    surface_fields,
    lateral_rate,
    vertical_rate,
    coupling_gain,
    send_slots,
    recv_slots,
    remap_weights,
):
    rows = lax.axis_size("comp")
    atmos = 3 * rows // 4
    levels = tracers.shape[1]
    chunks = levels // CHUNK
    cells = 2 * levels * 8
    f32, bf16, i32 = jnp.float32, jnp.bfloat16, jnp.int32
    hbm = pl.BlockSpec(memory_space=pltpu.HBM)
    dma = pltpu.SemaphoreType.DMA
    result = pl.pallas_call(
        functools.partial(kernel, levels),
        out_shape=jax.ShapeDtypeStruct((cells, 128), f32),
        in_specs=[hbm] * 8,
        out_specs=pl.BlockSpec(memory_space=pltpu.VMEM),
        scratch_shapes=[
            pltpu.VMEM((cells, 128), f32),
            pltpu.VMEM((cells, 128), f32),
            pltpu.VMEM((8, 128), bf16),
            pltpu.VMEM((levels - 1, 8, 128), bf16),
            pltpu.VMEM((levels + 1, 8, 128), f32),
            pltpu.VMEM((32, 128), f32),
            pltpu.VMEM((9, 8, 128), f32),
            pltpu.VMEM((atmos, 8, 128), f32),
            pltpu.VMEM((atmos, 8, 128), f32),
            pltpu.VMEM((64, atmos * 256), bf16),
            pltpu.VMEM((atmos, 256, 128), bf16),
            pltpu.VMEM((2, 8, 128), f32),
            pltpu.SMEM((2, 4), f32),
            pltpu.SMEM((2, rows), i32),
            pltpu.SMEM((2, rows), i32),
            pltpu.VMEM((2, 2, 2, levels, 128), f32),
            pltpu.VMEM((2, 2, 2, levels, 128), f32),
            pltpu.VMEM((2, chunks, 2, 8, 128), f32),
            pltpu.VMEM((2, chunks, 2, 8, 128), f32),
            pltpu.VMEM((2, 8, 128), f32),
            pltpu.VMEM((2, 8, 128), f32),
            pltpu.VMEM((2, 8, 128), f32),
            pltpu.VMEM((2, 8, 128), f32),
            dma((8,)),
            dma,
            dma,
            dma((2, 2, chunks)),
            dma((2, 2, chunks)),
            dma((2, 2, chunks)),
            dma((2, 2, chunks)),
            dma((2,)),
            dma((2,)),
            dma((2,)),
            dma((2,)),
        ],
        compiler_params=pltpu.CompilerParams(
            collective_id=0, has_side_effects=True, vmem_limit_bytes=60 * 1024 * 1024
        ),
        cost_estimate=pl.CostEstimate(
            flops=60_000_000, bytes_accessed=4_000_000, transcendentals=0
        ),
    )(
        tracers.reshape(cells, 128),
        surface_fields.reshape(32, 128),
        lateral_rate,
        vertical_rate,
        coupling_gain[0],
        jnp.transpose(send_slots[0, :, 0]),
        jnp.transpose(recv_slots[0, :, 0]),
        remap_weights.reshape(rows, 256, 128),
    )
    return result.reshape(tracers.shape)


def solution(mesh):
    return jax.shard_map(
        per_device,
        mesh=mesh,
        in_specs=(
            P(None, None, "tile", "comp"),
            P(None, "tile", "comp"),
            P("tile", "comp"),
            P(None, "tile", "comp"),
            P("comp", None, None),
            P("comp", None, "tile", None),
            P("comp", None, "tile", None),
            P("comp", None, "tile", None, None, None),
        ),
        out_specs=P(None, None, "tile", "comp"),
        check_vma=False,
    )
```

```python
import functools

import jax
import jax.numpy as jnp
from jax import lax
from jax.experimental import pallas as pl
from jax.experimental.pallas import tpu as pltpu
from jax.sharding import PartitionSpec as P

OLEV = 60
CHUNK = 24
RELAY = 2
MESH = pl.DeviceIdType.MESH


def tile_of(index):
    return pl.ds(pl.multiple_of(index * 8, 8), 8)


def kernel(
    levels,
    tracers,
    fields,
    lateral,
    vertical,
    gain,
    send_slots,
    recv_slots,
    weights,
    out,
    first,
    second,
    lat,
    ver,
    rate,
    surf,
    blocks,
    outgoing,
    incoming,
    spread,
    wts,
    forcing,
    gains,
    sends,
    recvs,
    x_out,
    x_in,
    y_out,
    y_in,
    x0_out,
    x0_in,
    y0_out,
    y0_in,
    load_sem,
    remap_send,
    remap_recv,
    x_send,
    x_recv,
    y_send,
    y_recv,
    x0_send,
    x0_recv,
    y0_send,
    y0_recv,
    here,
    near,
    go,
):
    rows = lax.axis_size("comp")
    tiles = lax.axis_size("tile")
    atmos = 3 * rows // 4
    ocean = rows - atmos
    row = lax.axis_index("comp")
    tile = lax.axis_index("tile")
    left = lax.rem(tile + tiles - 1, tiles)
    right = lax.rem(tile + 1, tiles)
    is_ocean = row >= atmos
    is_atmos = row < atmos
    has_lower = jnp.logical_and(row != 0, row != atmos)
    has_upper = jnp.logical_and(row != atmos - 1, row != rows - 1)
    no_lower = jnp.logical_or(row == 0, row == atmos)
    no_upper = jnp.logical_or(row == atmos - 1, row == rows - 1)
    live_levels = jnp.where(is_ocean, OLEV, levels)
    chunks = levels // CHUNK
    lane = lax.broadcasted_iota(jnp.int32, (8, 128), 1)
    sub = lax.broadcasted_iota(jnp.int32, (8, 128), 0)

    loads = [
        pltpu.make_async_copy(source, target, load_sem.at[place])
        for place, (source, target) in enumerate(
            [
                (fields, surf),
                (send_slots, sends),
                (tracers, first),
                (vertical, ver),
                (lateral, lat),
                (recv_slots, recvs),
                (gain, gains),
            ]
        )
    ]
    get_fields, get_sends, get_tracers, get_vertical, get_lateral, get_recvs, get_gain = loads
    for load in loads:
        load.start()

    def get_weights(base, count):
        return pltpu.make_async_copy(
            weights.at[pl.ds(base, count)], wts.at[pl.ds(0, count)], load_sem.at[7]
        )

    @pl.when(is_ocean)
    def _():
        get_weights(0, atmos).start()

    @pl.when(is_atmos)
    def _():
        get_weights(atmos, ocean).start()

    barrier = pltpu.get_barrier_semaphore()

    def greet(to_row, to_tile):
        pl.semaphore_signal(barrier, inc=1, device_id=(to_row, to_tile), device_id_type=MESH)

    @pl.when(is_atmos)
    def _():
        for partner in range(atmos, rows):
            greet(partner, tile)
        greet(row, left)
        greet(row, right)

        @pl.when(has_lower)
        def _():
            greet(row - 1, tile)

        @pl.when(has_upper)
        def _():
            greet(row + 1, tile)

    def list_blocks():
        get_fields.wait()
        get_sends.wait()
        for block in range(8):
            picked = surf[pl.ds(block, 4, stride=8), :]
            blocks[block, 0:4, :] = picked
            blocks[block, 4:8, :] = picked
        blocks[8] = jnp.zeros((8, 128), jnp.float32)

    def fill(base, place):
        slot0 = sends[0, base + place]
        slot1 = sends[1, base + place]
        slot0 = jnp.where(slot0 < 0, 8, slot0)
        slot1 = jnp.where(slot1 < 0, 8, slot1)
        outgoing[place] = jnp.where(sub < 4, blocks[slot0], blocks[slot1])

    def send_block(base, place, own_base):
        pltpu.make_async_remote_copy(
            src_ref=outgoing.at[place],
            dst_ref=incoming.at[row - own_base],
            send_sem=remap_send,
            recv_sem=remap_recv,
            device_id=(base + place, tile),
            device_id_type=MESH,
        ).start()

    @pl.when(is_ocean)
    def _():
        list_blocks()
        pl.semaphore_wait(barrier, atmos)
        pl.semaphore_signal(here, inc=1, device_id=(RELAY, tile), device_id_type=MESH)
        for place in range(atmos):
            fill(0, place)
            send_block(0, place, atmos)

    @pl.when(is_atmos)
    def _():
        list_blocks()
        for place in range(ocean):
            fill(atmos, place)
        pl.semaphore_wait(
            barrier, 2 + has_lower.astype(jnp.int32) + has_upper.astype(jnp.int32)
        )

    def pack_x(step, chunk, source):
        for var in range(2):
            start = (var * levels + chunk * CHUNK) * 8
            here = pl.ds(pl.multiple_of(chunk * CHUNK, 8), CHUNK)
            x_out[step, 1, var, here, :] = source[pl.ds(start, CHUNK, stride=8), :]
            x_out[step, 0, var, here, :] = source[pl.ds(start + 7, CHUNK, stride=8), :]

    def add_lanes(low, high, value, entry):
        turned = pltpu.roll(value, 2 * entry, 1) if entry else value
        low = jnp.where(lane == 2 * entry, turned, low)
        high = jnp.where(lane == (2 * entry + 127) % 128, turned, high)
        return low, high

    def put_y(target, wall, low, high):
        target[1] = low
        target[0] = high

        @pl.when(no_lower)
        def _():
            wall[0] = pltpu.roll(low, 127, 1)

        @pl.when(no_upper)
        def _():
            wall[1] = pltpu.roll(high, 1, 1)

    def copy_x(step, chunk, side):
        here = pl.ds(pl.multiple_of(chunk * CHUNK, 8), CHUNK)
        return pltpu.make_async_remote_copy(
            src_ref=x_out.at[step, side, :, here, :],
            dst_ref=x_in.at[step, side, :, here, :],
            send_sem=x_send.at[step, side, chunk],
            recv_sem=x_recv.at[step, side, chunk],
            device_id=(row, left if side else right),
            device_id_type=MESH,
        )

    def copy_y(step, chunk, side):
        return pltpu.make_async_remote_copy(
            src_ref=y_out.at[step, chunk, side],
            dst_ref=y_in.at[step, chunk, side],
            send_sem=y_send.at[step, side, chunk],
            recv_sem=y_recv.at[step, side, chunk],
            device_id=(row - 1 if side else row + 1, tile),
            device_id_type=MESH,
        )

    def copy_x0(side):
        return pltpu.make_async_remote_copy(
            src_ref=x0_out.at[side],
            dst_ref=x0_in.at[side],
            send_sem=x0_send.at[side],
            recv_sem=x0_recv.at[side],
            device_id=(row, left if side else right),
            device_id_type=MESH,
        )

    def copy_y0(side):
        return pltpu.make_async_remote_copy(
            src_ref=y0_out.at[side],
            dst_ref=y0_in.at[side],
            send_sem=y0_send.at[side],
            recv_sem=y0_recv.at[side],
            device_id=(row - 1 if side else row + 1, tile),
            device_id_type=MESH,
        )

    def start_edges(step, chunk):
        copy_x(step, chunk, 0).start()
        copy_x(step, chunk, 1).start()

        @pl.when(has_lower)
        def _():
            copy_y(step, chunk, 1).start()

        @pl.when(has_upper)
        def _():
            copy_y(step, chunk, 0).start()

    def await_edges(step, chunk):
        copy_x(step, chunk, 0).wait_recv()
        copy_x(step, chunk, 1).wait_recv()

        @pl.when(has_lower)
        def _():
            copy_y(step, chunk, 0).wait_recv()

        @pl.when(has_upper)
        def _():
            copy_y(step, chunk, 1).wait_recv()

    def end_edges(step, chunk):
        copy_x(step, chunk, 0).wait_send()
        copy_x(step, chunk, 1).wait_send()

        @pl.when(has_lower)
        def _():
            copy_y(step, chunk, 1).wait_send()

        @pl.when(has_upper)
        def _():
            copy_y(step, chunk, 0).wait_send()

    get_tracers.wait()

    def pack_first(turn, carry):
        chunk = chunks - 1 - turn
        pack_x(0, chunk, first)
        low = high = jnp.zeros((8, 128), jnp.float32)
        for level in range(CHUNK):
            for var in range(2):
                value = first[tile_of(var * levels + chunk * CHUNK + level), :]
                low, high = add_lanes(low, high, value, 2 * level + var)
        put_y(y_out.at[0, chunk], y_in.at[0, chunk], low, high)
        return carry

    lax.fori_loop(0, chunks, pack_first, 0)

    def await_blocks(count):
        pltpu.make_async_copy(
            incoming.at[pl.ds(0, count)], incoming.at[pl.ds(0, count)], remap_recv
        ).wait()

    @pl.when(is_ocean)
    def _():
        pl.semaphore_wait(go, 1)

    def send_first(turn, carry):
        start_edges(0, chunks - 1 - turn)
        return carry

    lax.fori_loop(0, chunks, send_first, 0)

    get_vertical.wait()
    get_lateral.wait()
    rate[0] = jnp.zeros((8, 128), jnp.float32)
    rate[levels] = jnp.zeros((8, 128), jnp.float32)

    def one_rate(level, carry):
        value = ver[level].astype(jnp.float32)
        rate[level + 1] = jnp.where(level + 1 < live_levels, value, 0.0)
        return carry

    lax.fori_loop(0, levels - 1, one_rate, 0, unroll=8)

    def sides_of(value, x_low, x_high, merged, entry):
        ends = pltpu.roll(merged, 127 - 2 * entry, 1)
        return (
            jnp.where(sub == 0, x_low, pltpu.roll(value, 1, 0))
            + jnp.where(sub == 7, x_high, pltpu.roll(value, 7, 0))
        ) + (
            jnp.where(lane == 0, ends, pltpu.roll(value, 1, 1))
            + jnp.where(lane == 127, ends, pltpu.roll(value, 127, 1))
        )

    def advance(step, chunk, source, target, merged, edges):
        lateral_here = lat[...].astype(jnp.float32)
        base = chunk * CHUNK
        previous = [None, None]
        centre = [None, None]
        low = high = jnp.zeros((8, 128), jnp.float32)
        for var in range(2):
            centre[var] = source[tile_of(var * levels + base), :]
            above = source[tile_of(var * levels + jnp.maximum(base - 1, 0)), :]
            previous[var] = rate[base] * (centre[var] - above)
        for level in range(CHUNK):
            here = base + level
            mixing = rate[here + 1]
            spreading = jnp.where(here < live_levels, lateral_here, 0.0)
            for var in range(2):
                entry = 2 * level + var
                after = jnp.minimum(here + 1, levels - 1) if level == CHUNK - 1 else here + 1
                value = centre[var]
                below = source[tile_of(var * levels + after), :]
                x_low = jnp.broadcast_to(x_in[step, 0, var, pl.ds(here, 1), :], (8, 128))
                x_high = jnp.broadcast_to(x_in[step, 1, var, pl.ds(here, 1), :], (8, 128))
                sides = sides_of(value, x_low, x_high, merged, entry)
                down = mixing * (below - value)
                result = value + spreading * (sides - 4.0 * value) + (down - previous[var])
                target[tile_of(var * levels + here), :] = result
                if edges:
                    low, high = add_lanes(low, high, result, entry)
                centre[var] = below
                previous[var] = down
        return low, high

    def merge(low, high):
        return jnp.where(lane % 2 == 1, pltpu.roll(low, 2, 1), high)

    def step_one(turn, carry):
        chunk = chunks - 1 - turn
        await_edges(0, chunk)
        merged = merge(y_in[0, chunk, 0], y_in[0, chunk, 1])
        low, high = advance(0, chunk, first, second, merged, True)
        pack_x(1, chunk, second)
        put_y(y_out.at[1, chunk], y_in.at[1, chunk], low, high)
        start_edges(1, chunk)
        return carry


    get_recvs.wait()
    get_gain.wait()

    def remap(base, count):
        def one(place, carry):
            for slot in range(2):
                lands = sub == recvs[slot, base + place]
                column = pl.ds(pl.multiple_of((place * 2 + slot) * 128, 128), 128)
                for pair in range(2):
                    value = jnp.concatenate(
                        [
                            jnp.where(
                                lands,
                                jnp.broadcast_to(
                                    incoming[place, slot * 4 + field : slot * 4 + field + 1, :],
                                    (8, 128),
                                ),
                                0.0,
                            )
                            for field in (2 * pair, 2 * pair + 1)
                        ],
                        axis=0,
                    )
                    coarse = value.astype(jnp.bfloat16)
                    fine = (value - coarse.astype(jnp.float32)).astype(jnp.bfloat16)
                    spread[16 * pair : 16 * pair + 16, column] = coarse
                    spread[32 + 16 * pair : 48 + 16 * pair, column] = fine
            return carry

        lax.fori_loop(0, count, one, 0, unroll=2)
        get_weights(base, count).wait()
        total = jnp.dot(
            spread[:, : count * 256],
            wts[:count].reshape(count * 256, 128),
            preferred_element_type=jnp.float32,
        )
        remapped = total[:32] + total[32:]
        low = high = jnp.zeros((8, 128), jnp.float32)
        values = []
        for var in range(2):
            force = gains[var, 0] * remapped[:8]
            for field in range(1, 4):
                force = force + gains[var, field] * remapped[8 * field : 8 * field + 8]
            forcing[var] = force
            low, high = add_lanes(low, high, force, var)
            values.append(force)
        x0_out[1] = jnp.where(sub == 0, values[0][0:1, :], values[1][0:1, :])
        x0_out[0] = jnp.where(sub == 0, values[0][7:8, :], values[1][7:8, :])
        put_y(y0_out, y0_in, low, high)

    def force():
        @pl.when(row == RELAY)
        def _():
            pl.semaphore_wait(here, ocean)
            for side in (left, right):
                pl.semaphore_signal(near, inc=1, device_id=(row, side), device_id_type=MESH)
            pl.semaphore_wait(near, 2)
            for partner in range(atmos, rows):
                pl.semaphore_signal(go, inc=1, device_id=(partner, tile), device_id_type=MESH)

        @pl.when(is_atmos)
        def _():
            await_blocks(ocean)
            remap(atmos, ocean)

        @pl.when(is_ocean)
        def _():
            await_blocks(atmos)
            remap(0, atmos)

        copy_x0(0).start()
        copy_x0(1).start()

        @pl.when(has_lower)
        def _():
            copy_y0(1).start()

        @pl.when(has_upper)
        def _():
            copy_y0(0).start()

        @pl.when(is_atmos)
        def _():
            for place in range(ocean):
                send_block(atmos, place, 0)

    forced_first = jnp.logical_and(row >= 2 * atmos // 3, is_atmos)
    steps_first = jnp.where(forced_first, 1, 0)

    def phase(turn, carry):
        @pl.when(turn == steps_first)
        def _():
            lax.fori_loop(0, chunks, step_one, 0)

        @pl.when(turn != steps_first)
        def _():
            force()

        return carry

    lax.fori_loop(0, 2, phase, 0)

    def step_two(turn, carry):
        chunk = chunks - 1 - turn
        await_edges(1, chunk)
        merged = merge(y_in[1, chunk, 0], y_in[1, chunk, 1])
        advance(1, chunk, second, out, merged, False)
        return carry

    lax.fori_loop(0, chunks, step_two, 0)
    for step in range(2):

        def end(chunk, carry):
            end_edges(step, chunk)
            return carry

        lax.fori_loop(0, chunks, end, 0)

    copy_x0(0).wait_recv()
    copy_x0(1).wait_recv()

    @pl.when(has_lower)
    def _():
        copy_y0(0).wait_recv()

    @pl.when(has_upper)
    def _():
        copy_y0(1).wait_recv()

    merged = merge(y0_in[0], y0_in[1])
    for var in range(2):
        force = forcing[var]
        x_low = jnp.broadcast_to(x0_in[0, var : var + 1, :], (8, 128))
        x_high = jnp.broadcast_to(x0_in[1, var : var + 1, :], (8, 128))
        mixing = rate[1] * force
        effect = lat[...].astype(jnp.float32) * (
            sides_of(force, x_low, x_high, merged, var) - 4.0 * force
        )
        out[tile_of(var * levels), :] += 2.0 * force + (effect - mixing)
        out[tile_of(var * levels + 1), :] += mixing

    copy_x0(0).wait_send()
    copy_x0(1).wait_send()

    @pl.when(has_lower)
    def _():
        copy_y0(1).wait_send()

    @pl.when(has_upper)
    def _():
        copy_y0(0).wait_send()

    @pl.when(is_ocean)
    def _():
        pltpu.make_async_copy(
            outgoing.at[pl.ds(0, atmos)], outgoing.at[pl.ds(0, atmos)], remap_send
        ).wait()

    @pl.when(is_atmos)
    def _():
        pltpu.make_async_copy(
            outgoing.at[pl.ds(0, ocean)], outgoing.at[pl.ds(0, ocean)], remap_send
        ).wait()


def per_device(
    tracers,
    surface_fields,
    lateral_rate,
    vertical_rate,
    coupling_gain,
    send_slots,
    recv_slots,
    remap_weights,
):
    rows = lax.axis_size("comp")
    atmos = 3 * rows // 4
    levels = tracers.shape[1]
    chunks = levels // CHUNK
    cells = 2 * levels * 8
    f32, bf16, i32 = jnp.float32, jnp.bfloat16, jnp.int32
    hbm = pl.BlockSpec(memory_space=pltpu.HBM)
    dma = pltpu.SemaphoreType.DMA
    result = pl.pallas_call(
        functools.partial(kernel, levels),
        out_shape=pltpu.VMEM((cells, 128), f32),
        in_specs=[hbm] * 8,
        out_specs=pl.BlockSpec(memory_space=pltpu.VMEM),
        scratch_shapes=[
            pltpu.VMEM((cells, 128), f32),
            pltpu.VMEM((cells, 128), f32),
            pltpu.VMEM((8, 128), bf16),
            pltpu.VMEM((levels - 1, 8, 128), bf16),
            pltpu.VMEM((levels + 1, 8, 128), f32),
            pltpu.VMEM((32, 128), f32),
            pltpu.VMEM((9, 8, 128), f32),
            pltpu.VMEM((atmos, 8, 128), f32),
            pltpu.VMEM((atmos, 8, 128), f32),
            pltpu.VMEM((64, atmos * 256), bf16),
            pltpu.VMEM((atmos, 256, 128), bf16),
            pltpu.VMEM((2, 8, 128), f32),
            pltpu.SMEM((2, 4), f32),
            pltpu.SMEM((2, rows), i32),
            pltpu.SMEM((2, rows), i32),
            pltpu.VMEM((2, 2, 2, levels, 128), f32),
            pltpu.VMEM((2, 2, 2, levels, 128), f32),
            pltpu.VMEM((2, chunks, 2, 8, 128), f32),
            pltpu.VMEM((2, chunks, 2, 8, 128), f32),
            pltpu.VMEM((2, 8, 128), f32),
            pltpu.VMEM((2, 8, 128), f32),
            pltpu.VMEM((2, 8, 128), f32),
            pltpu.VMEM((2, 8, 128), f32),
            dma((8,)),
            dma,
            dma,
            dma((2, 2, chunks)),
            dma((2, 2, chunks)),
            dma((2, 2, chunks)),
            dma((2, 2, chunks)),
            dma((2,)),
            dma((2,)),
            dma((2,)),
            dma((2,)),
            pltpu.SemaphoreType.REGULAR,
            pltpu.SemaphoreType.REGULAR,
            pltpu.SemaphoreType.REGULAR,
        ],
        compiler_params=pltpu.CompilerParams(
            collective_id=0, has_side_effects=True, vmem_limit_bytes=48 * 1024 * 1024
        ),
        cost_estimate=pl.CostEstimate(
            flops=60_000_000, bytes_accessed=4_000_000, transcendentals=0
        ),
    )(
        *[
            pltpu.with_memory_space_constraint(array, pltpu.HBM)
            for array in (
                tracers.reshape(cells, 128),
                surface_fields.reshape(32, 128),
                lateral_rate,
                vertical_rate,
                coupling_gain[0],
                jnp.transpose(send_slots[0, :, 0]),
                jnp.transpose(recv_slots[0, :, 0]),
                remap_weights.reshape(rows, 256, 128),
            )
        ]
    )
    return result.reshape(tracers.shape)


def solution(mesh):
    return jax.shard_map(
        per_device,
        mesh=mesh,
        in_specs=(
            P(None, None, "tile", "comp"),
            P(None, "tile", "comp"),
            P("tile", "comp"),
            P(None, "tile", "comp"),
            P("comp", None, None),
            P("comp", None, "tile", None),
            P("comp", None, "tile", None),
            P("comp", None, "tile", None, None, None),
        ),
        out_specs=P(None, None, "tile", "comp"),
        check_vma=False,
    )
```

```python
import functools

import jax
import jax.numpy as jnp
from jax import lax
from jax.experimental import pallas as pl
from jax.experimental.pallas import tpu as pltpu
from jax.sharding import PartitionSpec as P

OLEV = 60
CHUNK = 24
MESH = pl.DeviceIdType.MESH


def tile_of(index):
    return pl.ds(pl.multiple_of(index * 8, 8), 8)


def kernel(
    levels,
    tracers,
    fields,
    lateral,
    vertical,
    gain,
    send_slots,
    recv_slots,
    weights,
    out,
    first,
    second,
    lat,
    ver,
    rate,
    surf,
    blocks,
    outgoing,
    incoming,
    spread,
    wts,
    forcing,
    gains,
    sends,
    recvs,
    x_out,
    x_in,
    y_out,
    y_in,
    x0_out,
    x0_in,
    y0_out,
    y0_in,
    load_sem,
    remap_send,
    remap_recv,
    x_send,
    x_recv,
    y_send,
    y_recv,
    x0_send,
    x0_recv,
    y0_send,
    y0_recv,
    here,
    go,
):
    rows = lax.axis_size("comp")
    tiles = lax.axis_size("tile")
    atmos = 3 * rows // 4
    ocean = rows - atmos
    row = lax.axis_index("comp")
    tile = lax.axis_index("tile")
    left = lax.rem(tile + tiles - 1, tiles)
    right = lax.rem(tile + 1, tiles)
    is_ocean = row >= atmos
    is_atmos = row < atmos
    has_lower = jnp.logical_and(row != 0, row != atmos)
    has_upper = jnp.logical_and(row != atmos - 1, row != rows - 1)
    no_lower = jnp.logical_or(row == 0, row == atmos)
    no_upper = jnp.logical_or(row == atmos - 1, row == rows - 1)
    live_levels = jnp.where(is_ocean, OLEV, levels)
    chunks = levels // CHUNK
    lane = lax.broadcasted_iota(jnp.int32, (8, 128), 1)
    sub = lax.broadcasted_iota(jnp.int32, (8, 128), 0)

    loads = [
        pltpu.make_async_copy(source, target, load_sem.at[place])
        for place, (source, target) in enumerate(
            [
                (fields, surf),
                (send_slots, sends),
                (tracers, first),
                (vertical, ver),
                (lateral, lat),
                (recv_slots, recvs),
                (gain, gains),
            ]
        )
    ]
    get_fields, get_sends, get_tracers, get_vertical, get_lateral, get_recvs, get_gain = loads
    get_fields.start()
    get_sends.start()

    def get_weights(base, count):
        return pltpu.make_async_copy(
            weights.at[pl.ds(base, count)], wts.at[pl.ds(0, count)], load_sem.at[7]
        )

    barrier = pltpu.get_barrier_semaphore()

    def greet(to_row, to_tile):
        pl.semaphore_signal(barrier, inc=1, device_id=(to_row, to_tile), device_id_type=MESH)

    @pl.when(is_atmos)
    def _():
        for partner in range(atmos, rows):
            greet(partner, tile)
        greet(row, left)
        greet(row, right)

        @pl.when(has_lower)
        def _():
            greet(row - 1, tile)

        @pl.when(has_upper)
        def _():
            greet(row + 1, tile)

    half = tiles // 2
    odd = lax.rem(tile, 2) == 1
    even = lax.rem(tile, 2) == 0
    inner_left = jnp.logical_and(tile != 0, tile != half)
    inner_right = jnp.logical_and(tile != half - 1, tile != tiles - 1)
    first_of_left = jnp.logical_or(tile == 0, jnp.logical_and(odd, inner_left))
    first_of_right = jnp.logical_and(odd, inner_right)
    second_of_left = jnp.logical_and(even, inner_left)
    second_of_right = jnp.logical_or(tile == tiles - 1, jnp.logical_and(even, inner_right))
    middle = jnp.logical_or(tile == half - 1, tile == half)
    across = 2 * half - 1 - tile
    share = max(ocean // 2, 1)
    helper = lax.rem(row - atmos, share)
    helps = jnp.logical_and(row < share, middle)

    @pl.when(helps)
    def _():
        for turn in range(ocean // share):
            greet(atmos + turn * share + row, across)

    @pl.when(is_ocean)
    def _():
        @pl.when(first_of_left)
        def _():
            greet(row, left)

        @pl.when(first_of_right)
        def _():
            greet(row, right)

        @pl.when(has_upper)
        def _():
            greet(row + 1, tile)

    def release():
        def free(to_row, to_tile):
            pl.semaphore_signal(go, inc=1, device_id=(to_row, to_tile), device_id_type=MESH)

        @pl.when(second_of_right)
        def _():
            free(row, right)

        @pl.when(second_of_left)
        def _():
            free(row, left)

        @pl.when(has_lower)
        def _():
            free(row - 1, tile)

    for load in (get_tracers, get_vertical, get_lateral, get_recvs, get_gain):
        load.start()

    @pl.when(is_ocean)
    def _():
        get_weights(0, atmos).start()

    @pl.when(is_atmos)
    def _():
        get_weights(atmos, ocean).start()

    def list_blocks():
        get_fields.wait()
        get_sends.wait()
        for block in range(8):
            picked = surf[pl.ds(block, 4, stride=8), :]
            blocks[block, 0:4, :] = picked
            blocks[block, 4:8, :] = picked
        blocks[8] = jnp.zeros((8, 128), jnp.float32)

    def fill(base, place):
        slot0 = sends[0, base + place]
        slot1 = sends[1, base + place]
        slot0 = jnp.where(slot0 < 0, 8, slot0)
        slot1 = jnp.where(slot1 < 0, 8, slot1)
        outgoing[place] = jnp.where(sub < 4, blocks[slot0], blocks[slot1])

    def send_block(base, place, own_base):
        pltpu.make_async_remote_copy(
            src_ref=outgoing.at[place],
            dst_ref=incoming.at[row - own_base],
            send_sem=remap_send,
            recv_sem=remap_recv.at[row - own_base],
            device_id=(base + place, tile),
            device_id_type=MESH,
        ).start()

    @pl.when(is_ocean)
    def _():
        list_blocks()
        pl.semaphore_wait(
            barrier,
            atmos
            + second_of_left.astype(jnp.int32)
            + second_of_right.astype(jnp.int32)
            + has_lower.astype(jnp.int32)
            + middle.astype(jnp.int32),
        )

        @pl.when(middle)
        def _():
            pl.semaphore_signal(here, inc=1, device_id=(helper, across), device_id_type=MESH)

        for place in range(atmos):
            if place == atmos // 3:
                release()
            fill(0, place)
            send_block(0, place, atmos)

    @pl.when(is_atmos)
    def _():
        list_blocks()
        for place in range(ocean):
            fill(atmos, place)
        pl.semaphore_wait(
            barrier, 2 + has_lower.astype(jnp.int32) + has_upper.astype(jnp.int32)
        )

    def pack_x(step, chunk, source):
        for var in range(2):
            start = (var * levels + chunk * CHUNK) * 8
            here = pl.ds(pl.multiple_of(chunk * CHUNK, 8), CHUNK)
            x_out[step, 1, var, here, :] = source[pl.ds(start, CHUNK, stride=8), :]
            x_out[step, 0, var, here, :] = source[pl.ds(start + 7, CHUNK, stride=8), :]

    def add_lanes(low, high, value, entry):
        turned = pltpu.roll(value, 2 * entry, 1) if entry else value
        low = jnp.where(lane == 2 * entry, turned, low)
        high = jnp.where(lane == (2 * entry + 127) % 128, turned, high)
        return low, high

    def put_y(target, wall, low, high):
        target[1] = low
        target[0] = high

        @pl.when(no_lower)
        def _():
            wall[0] = pltpu.roll(low, 127, 1)

        @pl.when(no_upper)
        def _():
            wall[1] = pltpu.roll(high, 1, 1)

    def copy_x(step, chunk, side):
        here = pl.ds(pl.multiple_of(chunk * CHUNK, 8), CHUNK)
        return pltpu.make_async_remote_copy(
            src_ref=x_out.at[step, side, :, here, :],
            dst_ref=x_in.at[step, side, :, here, :],
            send_sem=x_send.at[step, side, chunk],
            recv_sem=x_recv.at[step, side, chunk],
            device_id=(row, left if side else right),
            device_id_type=MESH,
        )

    def copy_y(step, chunk, side):
        return pltpu.make_async_remote_copy(
            src_ref=y_out.at[step, chunk, side],
            dst_ref=y_in.at[step, chunk, side],
            send_sem=y_send.at[step, side, chunk],
            recv_sem=y_recv.at[step, side, chunk],
            device_id=(row - 1 if side else row + 1, tile),
            device_id_type=MESH,
        )

    def copy_x0(side):
        return pltpu.make_async_remote_copy(
            src_ref=x0_out.at[side],
            dst_ref=x0_in.at[side],
            send_sem=x0_send.at[side],
            recv_sem=x0_recv.at[side],
            device_id=(row, left if side else right),
            device_id_type=MESH,
        )

    def copy_y0(side):
        return pltpu.make_async_remote_copy(
            src_ref=y0_out.at[side],
            dst_ref=y0_in.at[side],
            send_sem=y0_send.at[side],
            recv_sem=y0_recv.at[side],
            device_id=(row - 1 if side else row + 1, tile),
            device_id_type=MESH,
        )

    def start_edges(step, chunk):
        copy_x(step, chunk, 0).start()
        copy_x(step, chunk, 1).start()

        @pl.when(has_lower)
        def _():
            copy_y(step, chunk, 1).start()

        @pl.when(has_upper)
        def _():
            copy_y(step, chunk, 0).start()

    def await_edges(step, chunk):
        copy_x(step, chunk, 0).wait_recv()
        copy_x(step, chunk, 1).wait_recv()

        @pl.when(has_lower)
        def _():
            copy_y(step, chunk, 0).wait_recv()

        @pl.when(has_upper)
        def _():
            copy_y(step, chunk, 1).wait_recv()

    def end_edges(step, chunk):
        copy_x(step, chunk, 0).wait_send()
        copy_x(step, chunk, 1).wait_send()

        @pl.when(has_lower)
        def _():
            copy_y(step, chunk, 1).wait_send()

        @pl.when(has_upper)
        def _():
            copy_y(step, chunk, 0).wait_send()

    get_tracers.wait()

    def pack_first(turn, carry):
        chunk = chunks - 1 - turn
        pack_x(0, chunk, first)
        low = high = jnp.zeros((8, 128), jnp.float32)
        for level in range(CHUNK):
            for var in range(2):
                value = first[tile_of(var * levels + chunk * CHUNK + level), :]
                low, high = add_lanes(low, high, value, 2 * level + var)
        put_y(y_out.at[0, chunk], y_in.at[0, chunk], low, high)
        return carry

    lax.fori_loop(0, chunks, pack_first, 0)

    def await_blocks(place):
        pltpu.make_async_copy(
            incoming.at[place], incoming.at[place], remap_recv.at[place]
        ).wait()

    @pl.when(is_ocean)
    def _():
        releases = (
            first_of_left.astype(jnp.int32)
            + first_of_right.astype(jnp.int32)
            + has_upper.astype(jnp.int32)
            + middle.astype(jnp.int32)
        )

        @pl.when(releases > 0)
        def _():
            pl.semaphore_wait(go, releases)

    def send_first(turn, carry):
        start_edges(0, chunks - 1 - turn)
        return carry

    lax.fori_loop(0, chunks, send_first, 0)

    get_vertical.wait()
    get_lateral.wait()
    rate[0] = jnp.zeros((8, 128), jnp.float32)
    rate[levels] = jnp.zeros((8, 128), jnp.float32)

    def one_rate(level, carry):
        value = ver[level].astype(jnp.float32)
        rate[level + 1] = jnp.where(level + 1 < live_levels, value, 0.0)
        return carry

    lax.fori_loop(0, levels - 1, one_rate, 0, unroll=8)

    def sides_of(value, x_low, x_high, merged, entry):
        ends = pltpu.roll(merged, 127 - 2 * entry, 1)
        return (
            jnp.where(sub == 0, x_low, pltpu.roll(value, 1, 0))
            + jnp.where(sub == 7, x_high, pltpu.roll(value, 7, 0))
        ) + (
            jnp.where(lane == 0, ends, pltpu.roll(value, 1, 1))
            + jnp.where(lane == 127, ends, pltpu.roll(value, 127, 1))
        )

    def advance(step, chunk, source, target, merged, edges):
        lateral_here = lat[...].astype(jnp.float32)
        base = chunk * CHUNK
        previous = [None, None]
        centre = [None, None]
        low = high = jnp.zeros((8, 128), jnp.float32)
        for var in range(2):
            centre[var] = source[tile_of(var * levels + base), :]
            above = source[tile_of(var * levels + jnp.maximum(base - 1, 0)), :]
            previous[var] = rate[base] * (centre[var] - above)
        for level in range(CHUNK):
            here = base + level
            mixing = rate[here + 1]
            spreading = jnp.where(here < live_levels, lateral_here, 0.0)
            for var in range(2):
                entry = 2 * level + var
                after = jnp.minimum(here + 1, levels - 1) if level == CHUNK - 1 else here + 1
                value = centre[var]
                below = source[tile_of(var * levels + after), :]
                x_low = jnp.broadcast_to(x_in[step, 0, var, pl.ds(here, 1), :], (8, 128))
                x_high = jnp.broadcast_to(x_in[step, 1, var, pl.ds(here, 1), :], (8, 128))
                sides = sides_of(value, x_low, x_high, merged, entry)
                down = mixing * (below - value)
                result = value + spreading * (sides - 4.0 * value) + (down - previous[var])
                target[tile_of(var * levels + here), :] = result
                if edges:
                    low, high = add_lanes(low, high, result, entry)
                centre[var] = below
                previous[var] = down
        return low, high

    def merge(low, high):
        return jnp.where(lane % 2 == 1, pltpu.roll(low, 2, 1), high)

    def step_one(turn, carry):
        chunk = chunks - 1 - turn
        await_edges(0, chunk)
        merged = merge(y_in[0, chunk, 0], y_in[0, chunk, 1])
        low, high = advance(0, chunk, first, second, merged, True)
        pack_x(1, chunk, second)
        put_y(y_out.at[1, chunk], y_in.at[1, chunk], low, high)
        start_edges(1, chunk)
        return carry


    get_recvs.wait()
    get_gain.wait()

    def place_blocks(base, place):
        await_blocks(place)
        for slot in range(2):
            lands = sub == recvs[slot, base + place]
            column = pl.ds(pl.multiple_of((place * 2 + slot) * 128, 128), 128)
            for pair in range(2):
                value = jnp.concatenate(
                    [
                        jnp.where(
                            lands,
                            jnp.broadcast_to(
                                incoming[place, slot * 4 + field : slot * 4 + field + 1, :],
                                (8, 128),
                            ),
                            0.0,
                        )
                        for field in (2 * pair, 2 * pair + 1)
                    ],
                    axis=0,
                )
                coarse = value.astype(jnp.bfloat16)
                fine = (value - coarse.astype(jnp.float32)).astype(jnp.bfloat16)
                spread[16 * pair : 16 * pair + 16, column] = coarse
                spread[32 + 16 * pair : 48 + 16 * pair, column] = fine

    def product(start, count):
        return jnp.dot(
            spread[:, start * 256 : (start + count) * 256],
            wts[start : start + count].reshape(count * 256, 128),
            preferred_element_type=jnp.float32,
        )

    def force(total):
        remapped = total[:32] + total[32:]
        values = []
        for var in range(2):
            value = gains[var, 0] * remapped[:8]
            for field in range(1, 4):
                value = value + gains[var, field] * remapped[8 * field : 8 * field + 8]
            forcing[var] = value
            values.append(value)
        x0_out[0] = jnp.where(sub == 0, values[0][7:8, :], values[1][7:8, :])
        x0_out[1] = jnp.where(sub == 0, values[0][0:1, :], values[1][0:1, :])
        copy_x0(0).start()
        copy_x0(1).start()
        low = high = jnp.zeros((8, 128), jnp.float32)
        for var in range(2):
            low, high = add_lanes(low, high, values[var], var)
        put_y(y0_out, y0_in, low, high)

        @pl.when(has_lower)
        def _():
            copy_y0(1).start()

        @pl.when(has_upper)
        def _():
            copy_y0(0).start()

    def exchange():
        @pl.when(is_atmos)
        def _():
            get_weights(atmos, ocean).wait()
            total = jnp.zeros((64, 128), jnp.float32)
            part = max(ocean // 4, 1)
            for start in range(0, ocean, part):
                for place in range(start, start + part):
                    place_blocks(atmos, place)
                total = total + product(start, part)
            force(total)
            for place in range(ocean):
                send_block(atmos, place, 0)

            @pl.when(helps)
            def _():
                pl.semaphore_wait(here, ocean // share)
                for turn in range(ocean // share):
                    pl.semaphore_signal(
                        go,
                        inc=1,
                        device_id=(atmos + turn * share + row, tile),
                        device_id_type=MESH,
                    )

        @pl.when(is_ocean)
        def _():
            def one(place, carry):
                place_blocks(0, place)
                return carry

            lax.fori_loop(0, atmos, one, 0)
            get_weights(0, atmos).wait()
            force(product(0, atmos))

    forced_first = jnp.logical_and(row >= 2 * atmos // 3, is_atmos)
    steps_first = jnp.where(forced_first, 1, 0)

    def phase(turn, carry):
        @pl.when(turn == steps_first)
        def _():
            lax.fori_loop(0, chunks, step_one, 0)

        @pl.when(turn != steps_first)
        def _():
            exchange()

        return carry

    lax.fori_loop(0, 2, phase, 0)

    def step_two(turn, carry):
        chunk = chunks - 1 - turn
        await_edges(1, chunk)
        merged = merge(y_in[1, chunk, 0], y_in[1, chunk, 1])
        advance(1, chunk, second, out, merged, False)
        return carry

    lax.fori_loop(0, chunks, step_two, 0)
    for step in range(2):

        def end(chunk, carry):
            end_edges(step, chunk)
            return carry

        lax.fori_loop(0, chunks, end, 0)

    lateral_here = lat[...].astype(jnp.float32)
    for var in range(2):
        value = forcing[var]
        mixing = rate[1] * value
        out[tile_of(var * levels), :] += 2.0 * value - mixing - 4.0 * lateral_here * value
        out[tile_of(var * levels + 1), :] += mixing

    copy_x0(0).wait_send()
    copy_x0(1).wait_send()

    @pl.when(has_lower)
    def _():
        copy_y0(1).wait_send()
        copy_y0(0).wait_recv()

    @pl.when(has_upper)
    def _():
        copy_y0(0).wait_send()
        copy_y0(1).wait_recv()

    @pl.when(is_ocean)
    def _():
        pltpu.make_async_copy(
            outgoing.at[pl.ds(0, atmos)], outgoing.at[pl.ds(0, atmos)], remap_send
        ).wait()

    @pl.when(is_atmos)
    def _():
        pltpu.make_async_copy(
            outgoing.at[pl.ds(0, ocean)], outgoing.at[pl.ds(0, ocean)], remap_send
        ).wait()

    merged = merge(y0_in[0], y0_in[1])
    copy_x0(0).wait_recv()
    copy_x0(1).wait_recv()
    for var in range(2):
        x_low = jnp.broadcast_to(x0_in[0, var : var + 1, :], (8, 128))
        x_high = jnp.broadcast_to(x0_in[1, var : var + 1, :], (8, 128))
        out[tile_of(var * levels), :] += lateral_here * sides_of(
            forcing[var], x_low, x_high, merged, var
        )


def per_device(
    tracers,
    surface_fields,
    lateral_rate,
    vertical_rate,
    coupling_gain,
    send_slots,
    recv_slots,
    remap_weights,
):
    rows = lax.axis_size("comp")
    atmos = 3 * rows // 4
    levels = tracers.shape[1]
    chunks = levels // CHUNK
    cells = 2 * levels * 8
    f32, bf16, i32 = jnp.float32, jnp.bfloat16, jnp.int32
    hbm = pl.BlockSpec(memory_space=pltpu.HBM)
    dma = pltpu.SemaphoreType.DMA
    result = pl.pallas_call(
        functools.partial(kernel, levels),
        out_shape=pltpu.VMEM((cells, 128), f32),
        in_specs=[hbm] * 8,
        out_specs=pl.BlockSpec(memory_space=pltpu.VMEM),
        scratch_shapes=[
            pltpu.VMEM((cells, 128), f32),
            pltpu.VMEM((cells, 128), f32),
            pltpu.VMEM((8, 128), bf16),
            pltpu.VMEM((levels - 1, 8, 128), bf16),
            pltpu.VMEM((levels + 1, 8, 128), f32),
            pltpu.VMEM((32, 128), f32),
            pltpu.VMEM((9, 8, 128), f32),
            pltpu.VMEM((atmos, 8, 128), f32),
            pltpu.VMEM((atmos, 8, 128), f32),
            pltpu.VMEM((64, atmos * 256), bf16),
            pltpu.VMEM((atmos, 256, 128), bf16),
            pltpu.VMEM((2, 8, 128), f32),
            pltpu.SMEM((2, 4), f32),
            pltpu.SMEM((2, rows), i32),
            pltpu.SMEM((2, rows), i32),
            pltpu.VMEM((2, 2, 2, levels, 128), f32),
            pltpu.VMEM((2, 2, 2, levels, 128), f32),
            pltpu.VMEM((2, chunks, 2, 8, 128), f32),
            pltpu.VMEM((2, chunks, 2, 8, 128), f32),
            pltpu.VMEM((2, 8, 128), f32),
            pltpu.VMEM((2, 8, 128), f32),
            pltpu.VMEM((2, 8, 128), f32),
            pltpu.VMEM((2, 8, 128), f32),
            dma((8,)),
            dma,
            dma((atmos,)),
            dma((2, 2, chunks)),
            dma((2, 2, chunks)),
            dma((2, 2, chunks)),
            dma((2, 2, chunks)),
            dma((2,)),
            dma((2,)),
            dma((2,)),
            dma((2,)),
            pltpu.SemaphoreType.REGULAR,
            pltpu.SemaphoreType.REGULAR,
        ],
        compiler_params=pltpu.CompilerParams(
            collective_id=0, has_side_effects=True, vmem_limit_bytes=48 * 1024 * 1024
        ),
        cost_estimate=pl.CostEstimate(
            flops=60_000_000, bytes_accessed=4_000_000, transcendentals=0
        ),
    )(
        *[
            pltpu.with_memory_space_constraint(array, pltpu.HBM)
            for array in (
                tracers.reshape(cells, 128),
                surface_fields.reshape(32, 128),
                lateral_rate,
                vertical_rate,
                coupling_gain[0],
                jnp.transpose(send_slots[0, :, 0]),
                jnp.transpose(recv_slots[0, :, 0]),
                remap_weights.reshape(rows, 256, 128),
            )
        ]
    )
    return result.reshape(tracers.shape)


def solution(mesh):
    return jax.shard_map(
        per_device,
        mesh=mesh,
        in_specs=(
            P(None, None, "tile", "comp"),
            P(None, "tile", "comp"),
            P("tile", "comp"),
            P(None, "tile", "comp"),
            P("comp", None, None),
            P("comp", None, "tile", None),
            P("comp", None, "tile", None),
            P("comp", None, "tile", None, None, None),
        ),
        out_specs=P(None, None, "tile", "comp"),
        check_vma=False,
    )
```

```python
import functools

import jax
import jax.numpy as jnp
from jax import lax
from jax.experimental import pallas as pl
from jax.experimental.pallas import tpu as pltpu
from jax.sharding import PartitionSpec as P

OLEV = 60
CHUNK = 24
MESH = pl.DeviceIdType.MESH


def tile_of(index):
    return pl.ds(pl.multiple_of(index * 8, 8), 8)


def kernel(
    levels,
    tracers,
    fields,
    lateral,
    vertical,
    gain,
    send_slots,
    recv_slots,
    weights,
    out,
    first,
    second,
    lat,
    ver,
    rate,
    surf,
    blocks,
    outgoing,
    incoming,
    spread,
    wts,
    forcing,
    gains,
    sends,
    recvs,
    x_out,
    x_in,
    y_out,
    y_in,
    x0_out,
    x0_in,
    y0_out,
    y0_in,
    load_sem,
    remap_send,
    remap_recv,
    x_send,
    x_recv,
    y_send,
    y_recv,
    x0_send,
    x0_recv,
    y0_send,
    y0_recv,
    here,
    go,
):
    rows = lax.axis_size("comp")
    tiles = lax.axis_size("tile")
    atmos = 3 * rows // 4
    ocean = rows - atmos
    row = lax.axis_index("comp")
    tile = lax.axis_index("tile")
    left = lax.rem(tile + tiles - 1, tiles)
    right = lax.rem(tile + 1, tiles)
    is_ocean = row >= atmos
    is_atmos = row < atmos
    has_lower = jnp.logical_and(row != 0, row != atmos)
    has_upper = jnp.logical_and(row != atmos - 1, row != rows - 1)
    no_lower = jnp.logical_or(row == 0, row == atmos)
    no_upper = jnp.logical_or(row == atmos - 1, row == rows - 1)
    live_levels = jnp.where(is_ocean, OLEV, levels)
    chunks = levels // CHUNK
    lane = lax.broadcasted_iota(jnp.int32, (8, 128), 1)
    sub = lax.broadcasted_iota(jnp.int32, (8, 128), 0)

    loads = [
        pltpu.make_async_copy(source, target, load_sem.at[place])
        for place, (source, target) in enumerate(
            [
                (fields, surf.at[pl.ds(0, 32)]),
                (send_slots, sends),
                (tracers, first.at[pl.ds(0, 16 * levels)]),
                (vertical, ver),
                (lateral, lat),
                (recv_slots, recvs),
                (gain, gains),
            ]
        )
    ]
    get_fields, get_sends, get_tracers, get_vertical, get_lateral, get_recvs, get_gain = loads
    get_fields.start()
    get_sends.start()

    def get_weights(base, count):
        return pltpu.make_async_copy(
            weights.at[pl.ds(base, count)], wts.at[pl.ds(0, count)], load_sem.at[7]
        )

    barrier = pltpu.get_barrier_semaphore()

    def greet(to_row, to_tile):
        pl.semaphore_signal(barrier, inc=1, device_id=(to_row, to_tile), device_id_type=MESH)

    @pl.when(is_atmos)
    def _():
        for partner in range(atmos, rows):
            greet(partner, tile)
        greet(row, left)
        greet(row, right)

        @pl.when(has_lower)
        def _():
            greet(row - 1, tile)

        @pl.when(has_upper)
        def _():
            greet(row + 1, tile)

    half = tiles // 2
    odd = lax.rem(tile, 2) == 1
    even = lax.rem(tile, 2) == 0
    inner_left = jnp.logical_and(tile != 0, tile != half)
    inner_right = jnp.logical_and(tile != half - 1, tile != tiles - 1)
    first_of_left = jnp.logical_or(tile == 0, jnp.logical_and(odd, inner_left))
    first_of_right = jnp.logical_and(odd, inner_right)
    second_of_left = jnp.logical_and(even, inner_left)
    second_of_right = jnp.logical_or(tile == tiles - 1, jnp.logical_and(even, inner_right))
    middle = jnp.logical_or(tile == half - 1, tile == half)
    across = 2 * half - 1 - tile
    share = max(ocean // 2, 1)
    helper = lax.rem(row - atmos, share)
    helps = jnp.logical_and(row < share, middle)

    @pl.when(helps)
    def _():
        for turn in range(ocean // share):
            greet(atmos + turn * share + row, across)

    @pl.when(is_ocean)
    def _():
        @pl.when(first_of_left)
        def _():
            greet(row, left)

        @pl.when(first_of_right)
        def _():
            greet(row, right)

        @pl.when(has_upper)
        def _():
            greet(row + 1, tile)

    def release():
        def free(to_row, to_tile):
            pl.semaphore_signal(go, inc=1, device_id=(to_row, to_tile), device_id_type=MESH)

        @pl.when(second_of_right)
        def _():
            free(row, right)

        @pl.when(second_of_left)
        def _():
            free(row, left)

        @pl.when(has_lower)
        def _():
            free(row - 1, tile)

    for load in (get_tracers, get_vertical, get_lateral, get_recvs, get_gain):
        load.start()

    @pl.when(is_ocean)
    def _():
        get_weights(0, atmos).start()

    @pl.when(is_atmos)
    def _():
        get_weights(atmos, ocean).start()

    def list_blocks():
        get_fields.wait()
        get_sends.wait()
        for block in range(8):
            picked = surf[pl.ds(block, 4, stride=8), :]
            blocks[block, 0:4, :] = picked
            blocks[block, 4:8, :] = picked
        blocks[8] = jnp.zeros((8, 128), jnp.float32)

    def fill(base, place):
        slot0 = sends[0, base + place]
        slot1 = sends[1, base + place]
        slot0 = jnp.where(slot0 < 0, 8, slot0)
        slot1 = jnp.where(slot1 < 0, 8, slot1)
        outgoing[place] = jnp.where(sub < 4, blocks[slot0], blocks[slot1])

    def send_block(base, place, own_base):
        pltpu.make_async_remote_copy(
            src_ref=outgoing.at[place],
            dst_ref=incoming.at[row - own_base],
            send_sem=remap_send,
            recv_sem=remap_recv.at[row - own_base],
            device_id=(base + place, tile),
            device_id_type=MESH,
        ).start()

    @pl.when(is_ocean)
    def _():
        list_blocks()
        pl.semaphore_wait(
            barrier,
            atmos
            + second_of_left.astype(jnp.int32)
            + second_of_right.astype(jnp.int32)
            + has_lower.astype(jnp.int32)
            + middle.astype(jnp.int32),
        )

        @pl.when(middle)
        def _():
            pl.semaphore_signal(here, inc=1, device_id=(helper, across), device_id_type=MESH)

        for place in range(atmos):
            if place == atmos // 3:
                release()
            fill(0, place)
            send_block(0, place, atmos)

    @pl.when(is_atmos)
    def _():
        list_blocks()
        for place in range(ocean):
            fill(atmos, place)
        pl.semaphore_wait(
            barrier, 2 + has_lower.astype(jnp.int32) + has_upper.astype(jnp.int32)
        )

    def pack_x(step, chunk, source):
        for var in range(2):
            start = (var * levels + chunk * CHUNK) * 8
            here = pl.ds(pl.multiple_of(chunk * CHUNK, 8), CHUNK)
            x_out[step, 1, var, here, :] = source[pl.ds(start, CHUNK, stride=8), :]
            x_out[step, 0, var, here, :] = source[pl.ds(start + 7, CHUNK, stride=8), :]

    def add_lanes(low, high, value, entry):
        turned = pltpu.roll(value, 2 * entry, 1) if entry else value
        low = jnp.where(lane == 2 * entry, turned, low)
        high = jnp.where(lane == (2 * entry + 127) % 128, turned, high)
        return low, high

    def put_y(target, wall, low, high):
        target[1] = low
        target[0] = high

        @pl.when(no_lower)
        def _():
            wall[0] = pltpu.roll(low, 127, 1)

        @pl.when(no_upper)
        def _():
            wall[1] = pltpu.roll(high, 1, 1)

    def copy_x(step, chunk, side):
        here = pl.ds(pl.multiple_of(chunk * CHUNK, 8), CHUNK)
        return pltpu.make_async_remote_copy(
            src_ref=x_out.at[step, side, :, here, :],
            dst_ref=x_in.at[step, side, :, here, :],
            send_sem=x_send.at[step, side, chunk],
            recv_sem=x_recv.at[step, side, chunk],
            device_id=(row, left if side else right),
            device_id_type=MESH,
        )

    def copy_y(step, chunk, side):
        return pltpu.make_async_remote_copy(
            src_ref=y_out.at[step, chunk, side],
            dst_ref=y_in.at[step, chunk, side],
            send_sem=y_send.at[step, side, chunk],
            recv_sem=y_recv.at[step, side, chunk],
            device_id=(row - 1 if side else row + 1, tile),
            device_id_type=MESH,
        )

    def copy_x0(side):
        return pltpu.make_async_remote_copy(
            src_ref=x0_out.at[side],
            dst_ref=x0_in.at[side],
            send_sem=x0_send.at[side],
            recv_sem=x0_recv.at[side],
            device_id=(row, left if side else right),
            device_id_type=MESH,
        )

    def copy_y0(side):
        return pltpu.make_async_remote_copy(
            src_ref=y0_out.at[side],
            dst_ref=y0_in.at[side],
            send_sem=y0_send.at[side],
            recv_sem=y0_recv.at[side],
            device_id=(row - 1 if side else row + 1, tile),
            device_id_type=MESH,
        )

    def start_edges(step, chunk):
        copy_x(step, chunk, 0).start()
        copy_x(step, chunk, 1).start()

        @pl.when(has_lower)
        def _():
            copy_y(step, chunk, 1).start()

        @pl.when(has_upper)
        def _():
            copy_y(step, chunk, 0).start()

    def await_edges(step, chunk):
        copy_x(step, chunk, 0).wait_recv()
        copy_x(step, chunk, 1).wait_recv()

        @pl.when(has_lower)
        def _():
            copy_y(step, chunk, 0).wait_recv()

        @pl.when(has_upper)
        def _():
            copy_y(step, chunk, 1).wait_recv()

    def end_edges(step, chunk):
        copy_x(step, chunk, 0).wait_send()
        copy_x(step, chunk, 1).wait_send()

        @pl.when(has_lower)
        def _():
            copy_y(step, chunk, 1).wait_send()

        @pl.when(has_upper)
        def _():
            copy_y(step, chunk, 0).wait_send()

    get_tracers.wait()

    def pack_first(turn, carry):
        chunk = chunks - 1 - turn
        pack_x(0, chunk, first)
        low = high = jnp.zeros((8, 128), jnp.float32)
        for level in range(CHUNK):
            for var in range(2):
                value = first[tile_of(var * levels + chunk * CHUNK + level), :]
                low, high = add_lanes(low, high, value, 2 * level + var)
        put_y(y_out.at[0, chunk], y_in.at[0, chunk], low, high)
        return carry

    lax.fori_loop(0, chunks, pack_first, 0)

    def await_blocks(place):
        pltpu.make_async_copy(
            incoming.at[place], incoming.at[place], remap_recv.at[place]
        ).wait()

    @pl.when(is_ocean)
    def _():
        releases = (
            first_of_left.astype(jnp.int32)
            + first_of_right.astype(jnp.int32)
            + has_upper.astype(jnp.int32)
            + middle.astype(jnp.int32)
        )

        @pl.when(releases > 0)
        def _():
            pl.semaphore_wait(go, releases)

    def send_first(turn, carry):
        start_edges(0, chunks - 1 - turn)
        return carry

    lax.fori_loop(0, chunks, send_first, 0)

    get_vertical.wait()
    get_lateral.wait()
    rate[0] = jnp.zeros((8, 128), jnp.float32)
    rate[levels] = jnp.zeros((8, 128), jnp.float32)

    def one_rate(level, carry):
        value = ver[level].astype(jnp.float32)
        rate[level + 1] = jnp.where(level + 1 < live_levels, value, 0.0)
        return carry

    lax.fori_loop(0, levels - 1, one_rate, 0, unroll=8)

    def sides_of(value, x_low, x_high, merged, entry):
        ends = pltpu.roll(merged, 127 - 2 * entry, 1)
        return (
            jnp.where(sub == 0, x_low, pltpu.roll(value, 1, 0))
            + jnp.where(sub == 7, x_high, pltpu.roll(value, 7, 0))
        ) + (
            jnp.where(lane == 0, ends, pltpu.roll(value, 1, 1))
            + jnp.where(lane == 127, ends, pltpu.roll(value, 127, 1))
        )

    def advance(step, chunk, source, target, merged, edges):
        lateral_here = lat[...].astype(jnp.float32)
        base = chunk * CHUNK
        previous = [None, None]
        centre = [None, None]
        low = high = jnp.zeros((8, 128), jnp.float32)
        for var in range(2):
            centre[var] = source[tile_of(var * levels + base), :]
            above = source[tile_of(var * levels + jnp.maximum(base - 1, 0)), :]
            previous[var] = rate[base] * (centre[var] - above)
        for level in range(CHUNK):
            here = base + level
            mixing = rate[here + 1]
            spreading = jnp.where(here < live_levels, lateral_here, 0.0)
            for var in range(2):
                entry = 2 * level + var
                after = jnp.minimum(here + 1, levels - 1) if level == CHUNK - 1 else here + 1
                value = centre[var]
                below = source[tile_of(var * levels + after), :]
                x_low = jnp.broadcast_to(x_in[step, 0, var, pl.ds(here, 1), :], (8, 128))
                x_high = jnp.broadcast_to(x_in[step, 1, var, pl.ds(here, 1), :], (8, 128))
                sides = sides_of(value, x_low, x_high, merged, entry)
                down = mixing * (below - value)
                result = value + spreading * (sides - 4.0 * value) + (down - previous[var])
                target[tile_of(var * levels + here), :] = result
                if edges:
                    low, high = add_lanes(low, high, result, entry)
                centre[var] = below
                previous[var] = down
        return low, high

    def merge(low, high):
        return jnp.where(lane % 2 == 1, pltpu.roll(low, 2, 1), high)

    def step_one(turn, carry):
        chunk = chunks - 1 - turn
        await_edges(0, chunk)
        merged = merge(y_in[0, chunk, 0], y_in[0, chunk, 1])
        low, high = advance(0, chunk, first, second, merged, True)
        pack_x(1, chunk, second)
        put_y(y_out.at[1, chunk], y_in.at[1, chunk], low, high)
        start_edges(1, chunk)
        return carry


    get_recvs.wait()
    get_gain.wait()

    def place_blocks(base, place):
        await_blocks(place)
        for slot in range(2):
            lands = sub == recvs[slot, base + place]
            column = pl.ds(pl.multiple_of((place * 2 + slot) * 128, 128), 128)
            for pair in range(2):
                value = jnp.concatenate(
                    [
                        jnp.where(
                            lands,
                            jnp.broadcast_to(
                                incoming[place, slot * 4 + field : slot * 4 + field + 1, :],
                                (8, 128),
                            ),
                            0.0,
                        )
                        for field in (2 * pair, 2 * pair + 1)
                    ],
                    axis=0,
                )
                coarse = value.astype(jnp.bfloat16)
                fine = (value - coarse.astype(jnp.float32)).astype(jnp.bfloat16)
                spread[16 * pair : 16 * pair + 16, column] = coarse
                spread[32 + 16 * pair : 48 + 16 * pair, column] = fine

    def product(start, count):
        return jnp.dot(
            spread[:, start * 256 : (start + count) * 256],
            wts[start : start + count].reshape(count * 256, 128),
            preferred_element_type=jnp.float32,
        )

    def force(total):
        remapped = total[:32] + total[32:]
        values = []
        for var in range(2):
            value = gains[var, 0] * remapped[:8]
            for field in range(1, 4):
                value = value + gains[var, field] * remapped[8 * field : 8 * field + 8]
            forcing[var] = value
            values.append(value)
        x0_out[0] = jnp.where(sub == 0, values[0][7:8, :], values[1][7:8, :])
        x0_out[1] = jnp.where(sub == 0, values[0][0:1, :], values[1][0:1, :])
        copy_x0(0).start()
        copy_x0(1).start()
        low = high = jnp.zeros((8, 128), jnp.float32)
        for var in range(2):
            low, high = add_lanes(low, high, values[var], var)
        put_y(y0_out, y0_in, low, high)

        @pl.when(has_lower)
        def _():
            copy_y0(1).start()

        @pl.when(has_upper)
        def _():
            copy_y0(0).start()

    def exchange():
        @pl.when(is_atmos)
        def _():
            get_weights(atmos, ocean).wait()
            total = jnp.zeros((64, 128), jnp.float32)
            part = max(ocean // 4, 1)
            for start in range(0, ocean, part):
                for place in range(start, start + part):
                    place_blocks(atmos, place)
                total = total + product(start, part)
            force(total)
            for place in range(ocean):
                send_block(atmos, place, 0)

            @pl.when(helps)
            def _():
                pl.semaphore_wait(here, ocean // share)
                for turn in range(ocean // share):
                    pl.semaphore_signal(
                        go,
                        inc=1,
                        device_id=(atmos + turn * share + row, tile),
                        device_id_type=MESH,
                    )

        @pl.when(is_ocean)
        def _():
            def one(place, carry):
                place_blocks(0, place)
                return carry

            lax.fori_loop(0, atmos, one, 0)
            get_weights(0, atmos).wait()
            force(product(0, atmos))

    forced_first = jnp.logical_and(row >= 2 * atmos // 3, is_atmos)
    steps_first = jnp.where(forced_first, 1, 0)

    def phase(turn, carry):
        @pl.when(turn == steps_first)
        def _():
            lax.fori_loop(0, chunks, step_one, 0)

        @pl.when(turn != steps_first)
        def _():
            exchange()

        return carry

    lax.fori_loop(0, 2, phase, 0)

    def step_two(turn, carry):
        chunk = chunks - 1 - turn
        await_edges(1, chunk)
        merged = merge(y_in[1, chunk, 0], y_in[1, chunk, 1])
        advance(1, chunk, second, out, merged, False)
        return carry

    lax.fori_loop(0, chunks, step_two, 0)
    for step in range(2):

        def end(chunk, carry):
            end_edges(step, chunk)
            return carry

        lax.fori_loop(0, chunks, end, 0)

    lateral_here = lat[...].astype(jnp.float32)
    for var in range(2):
        value = forcing[var]
        mixing = rate[1] * value
        out[tile_of(var * levels), :] += 2.0 * value - mixing - 4.0 * lateral_here * value
        out[tile_of(var * levels + 1), :] += mixing

    copy_x0(0).wait_send()
    copy_x0(1).wait_send()

    @pl.when(has_lower)
    def _():
        copy_y0(1).wait_send()
        copy_y0(0).wait_recv()

    @pl.when(has_upper)
    def _():
        copy_y0(0).wait_send()
        copy_y0(1).wait_recv()

    @pl.when(is_ocean)
    def _():
        pltpu.make_async_copy(
            outgoing.at[pl.ds(0, atmos)], outgoing.at[pl.ds(0, atmos)], remap_send
        ).wait()

    @pl.when(is_atmos)
    def _():
        pltpu.make_async_copy(
            outgoing.at[pl.ds(0, ocean)], outgoing.at[pl.ds(0, ocean)], remap_send
        ).wait()

    merged = merge(y0_in[0], y0_in[1])
    copy_x0(0).wait_recv()
    copy_x0(1).wait_recv()
    for var in range(2):
        x_low = jnp.broadcast_to(x0_in[0, var : var + 1, :], (8, 128))
        x_high = jnp.broadcast_to(x0_in[1, var : var + 1, :], (8, 128))
        out[tile_of(var * levels), :] += lateral_here * sides_of(
            forcing[var], x_low, x_high, merged, var
        )


def per_device(
    tracers,
    surface_fields,
    lateral_rate,
    vertical_rate,
    coupling_gain,
    send_slots,
    recv_slots,
    remap_weights,
):
    rows = lax.axis_size("comp")
    atmos = 3 * rows // 4
    levels = tracers.shape[1]
    chunks = levels // CHUNK
    cells = 2 * levels * 8
    f32, bf16, i32 = jnp.float32, jnp.bfloat16, jnp.int32
    hbm = pl.BlockSpec(memory_space=pltpu.HBM)
    dma = pltpu.SemaphoreType.DMA
    result = pl.pallas_call(
        functools.partial(kernel, levels),
        out_shape=pltpu.VMEM((cells, 128), f32),
        in_specs=[hbm] * 8,
        out_specs=pl.BlockSpec(memory_space=pltpu.VMEM),
        scratch_shapes=[
            pltpu.VMEM((cells + 8, 128), f32),
            pltpu.VMEM((cells + 8, 128), f32),
            pltpu.VMEM((8, 128), bf16),
            pltpu.VMEM((levels - 1, 8, 128), bf16),
            pltpu.VMEM((levels + 1, 8, 128), f32),
            pltpu.VMEM((40, 128), f32),
            pltpu.VMEM((9, 8, 128), f32),
            pltpu.VMEM((atmos, 8, 128), f32),
            pltpu.VMEM((atmos, 8, 128), f32),
            pltpu.VMEM((64, atmos * 256), bf16),
            pltpu.VMEM((atmos, 256, 128), bf16),
            pltpu.VMEM((2, 8, 128), f32),
            pltpu.SMEM((2, 4), f32),
            pltpu.SMEM((2, rows), i32),
            pltpu.SMEM((2, rows), i32),
            pltpu.VMEM((2, 2, 2, levels, 128), f32),
            pltpu.VMEM((2, 2, 2, levels, 128), f32),
            pltpu.VMEM((2, chunks, 2, 8, 128), f32),
            pltpu.VMEM((2, chunks, 2, 8, 128), f32),
            pltpu.VMEM((2, 8, 128), f32),
            pltpu.VMEM((2, 8, 128), f32),
            pltpu.VMEM((2, 8, 128), f32),
            pltpu.VMEM((2, 8, 128), f32),
            dma((8,)),
            dma,
            dma((atmos,)),
            dma((2, 2, chunks)),
            dma((2, 2, chunks)),
            dma((2, 2, chunks)),
            dma((2, 2, chunks)),
            dma((2,)),
            dma((2,)),
            dma((2,)),
            dma((2,)),
            pltpu.SemaphoreType.REGULAR,
            pltpu.SemaphoreType.REGULAR,
        ],
        compiler_params=pltpu.CompilerParams(
            collective_id=0, has_side_effects=True, vmem_limit_bytes=48 * 1024 * 1024
        ),
        cost_estimate=pl.CostEstimate(
            flops=60_000_000, bytes_accessed=4_000_000, transcendentals=0
        ),
    )(
        *[
            pltpu.with_memory_space_constraint(array, pltpu.HBM)
            for array in (
                tracers.reshape(cells, 128),
                surface_fields.reshape(32, 128),
                lateral_rate,
                vertical_rate,
                coupling_gain[0],
                jnp.transpose(send_slots[0, :, 0]),
                jnp.transpose(recv_slots[0, :, 0]),
                remap_weights.reshape(rows, 256, 128),
            )
        ]
    )
    return result.reshape(tracers.shape)


def solution(mesh):
    return jax.shard_map(
        per_device,
        mesh=mesh,
        in_specs=(
            P(None, None, "tile", "comp"),
            P(None, "tile", "comp"),
            P("tile", "comp"),
            P(None, "tile", "comp"),
            P("comp", None, None),
            P("comp", None, "tile", None),
            P("comp", None, "tile", None),
            P("comp", None, "tile", None, None, None),
        ),
        out_specs=P(None, None, "tile", "comp"),
        check_vma=False,
    )
```

```python
import functools

import jax
import jax.numpy as jnp
from jax import lax
from jax.experimental import pallas as pl
from jax.experimental.pallas import tpu as pltpu
from jax.sharding import PartitionSpec as P

OLEV = 60
CHUNK = 24
MESH = pl.DeviceIdType.MESH


def tile_of(index):
    return pl.ds(pl.multiple_of(index * 8, 8), 8)


def kernel(
    levels,
    tracers,
    fields,
    lateral,
    vertical,
    gain,
    send_slots,
    recv_slots,
    weights,
    out,
    first,
    second,
    lat,
    ver,
    rate,
    surf,
    blocks,
    outgoing,
    incoming,
    spread,
    wts,
    forcing,
    gains,
    sends,
    recvs,
    x_out,
    x_in,
    y_out,
    y_in,
    x0_out,
    x0_in,
    y0_out,
    y0_in,
    load_sem,
    remap_send,
    remap_recv,
    x_send,
    x_recv,
    y_send,
    y_recv,
    x0_send,
    x0_recv,
    y0_send,
    y0_recv,
    here,
    go,
):
    rows = lax.axis_size("comp")
    tiles = lax.axis_size("tile")
    atmos = 3 * rows // 4
    ocean = rows - atmos
    row = lax.axis_index("comp")
    tile = lax.axis_index("tile")
    left = lax.rem(tile + tiles - 1, tiles)
    right = lax.rem(tile + 1, tiles)
    is_ocean = row >= atmos
    is_atmos = row < atmos
    has_lower = jnp.logical_and(row != 0, row != atmos)
    has_upper = jnp.logical_and(row != atmos - 1, row != rows - 1)
    no_lower = jnp.logical_or(row == 0, row == atmos)
    no_upper = jnp.logical_or(row == atmos - 1, row == rows - 1)
    live_levels = jnp.where(is_ocean, OLEV, levels)
    chunks = levels // CHUNK
    lane = lax.broadcasted_iota(jnp.int32, (8, 128), 1)
    sub = lax.broadcasted_iota(jnp.int32, (8, 128), 0)

    loads = [
        pltpu.make_async_copy(source, target, load_sem.at[place])
        for place, (source, target) in enumerate(
            [
                (fields, surf.at[pl.ds(0, 32)]),
                (send_slots, sends),
                (tracers, first.at[pl.ds(0, 16 * levels)]),
                (vertical, ver),
                (lateral, lat),
                (recv_slots, recvs),
                (gain, gains),
            ]
        )
    ]
    get_fields, get_sends, get_tracers, get_vertical, get_lateral, get_recvs, get_gain = loads
    get_fields.start()
    get_sends.start()

    def get_weights(base, count):
        return pltpu.make_async_copy(
            weights.at[pl.ds(base, count)], wts.at[pl.ds(0, count)], load_sem.at[7]
        )

    barrier = pltpu.get_barrier_semaphore()

    def greet(to_row, to_tile):
        pl.semaphore_signal(barrier, inc=1, device_id=(to_row, to_tile), device_id_type=MESH)

    @pl.when(is_atmos)
    def _():
        for partner in range(atmos, rows):
            greet(partner, tile)
        greet(row, left)
        greet(row, right)

        @pl.when(has_lower)
        def _():
            greet(row - 1, tile)

        @pl.when(has_upper)
        def _():
            greet(row + 1, tile)

    half = tiles // 2
    odd = lax.rem(tile, 2) == 1
    even = lax.rem(tile, 2) == 0
    inner_left = jnp.logical_and(tile != 0, tile != half)
    inner_right = jnp.logical_and(tile != half - 1, tile != tiles - 1)
    first_of_left = jnp.logical_or(tile == 0, jnp.logical_and(odd, inner_left))
    first_of_right = jnp.logical_and(odd, inner_right)
    second_of_left = jnp.logical_and(even, inner_left)
    second_of_right = jnp.logical_or(tile == tiles - 1, jnp.logical_and(even, inner_right))
    middle = jnp.logical_or(tile == half - 1, tile == half)
    across = 2 * half - 1 - tile
    share = max(ocean // 2, 1)
    helper = lax.rem(row - atmos, share)
    helps = jnp.logical_and(row < share, middle)

    @pl.when(helps)
    def _():
        for turn in range(ocean // share):
            greet(atmos + turn * share + row, across)

    @pl.when(is_ocean)
    def _():
        @pl.when(first_of_left)
        def _():
            greet(row, left)

        @pl.when(first_of_right)
        def _():
            greet(row, right)

        @pl.when(has_upper)
        def _():
            greet(row + 1, tile)

    def release():
        def free(to_row, to_tile):
            pl.semaphore_signal(go, inc=1, device_id=(to_row, to_tile), device_id_type=MESH)

        @pl.when(second_of_right)
        def _():
            free(row, right)

        @pl.when(second_of_left)
        def _():
            free(row, left)

        @pl.when(has_lower)
        def _():
            free(row - 1, tile)

    for load in (get_tracers, get_vertical, get_lateral, get_recvs, get_gain):
        load.start()

    @pl.when(is_ocean)
    def _():
        get_weights(0, atmos).start()

    @pl.when(is_atmos)
    def _():
        get_weights(atmos, ocean).start()

    def list_blocks():
        get_fields.wait()
        get_sends.wait()
        for block in range(8):
            picked = surf[pl.ds(block, 4, stride=8), :]
            blocks[block, 0:4, :] = picked
            blocks[block, 4:8, :] = picked
        blocks[8] = jnp.zeros((8, 128), jnp.float32)

    def fill(base, place):
        slot0 = sends[0, base + place]
        slot1 = sends[1, base + place]
        slot0 = jnp.where(slot0 < 0, 8, slot0)
        slot1 = jnp.where(slot1 < 0, 8, slot1)
        outgoing[place] = jnp.where(sub < 4, blocks[slot0], blocks[slot1])

    def send_block(base, place, own_base):
        pltpu.make_async_remote_copy(
            src_ref=outgoing.at[place],
            dst_ref=incoming.at[row - own_base],
            send_sem=remap_send,
            recv_sem=remap_recv.at[row - own_base],
            device_id=(base + place, tile),
            device_id_type=MESH,
        ).start()

    @pl.when(is_ocean)
    def _():
        list_blocks()
        pl.semaphore_wait(
            barrier,
            atmos
            + second_of_left.astype(jnp.int32)
            + second_of_right.astype(jnp.int32)
            + has_lower.astype(jnp.int32)
            + middle.astype(jnp.int32),
        )

        @pl.when(middle)
        def _():
            pl.semaphore_signal(here, inc=1, device_id=(helper, across), device_id_type=MESH)

        def one(turn, carry):
            step = lax.rem(turn, share)
            run = turn // share
            run = jnp.where(lax.rem(run, 2) == 0, run // 2, atmos // share - 1 - run // 2)
            place = run * share + jnp.where(2 * helper < share, share - 1 - step, step)
            fill(0, place)
            send_block(0, place, atmos)
            return carry

        lax.fori_loop(0, atmos // 3, one, 0)
        release()
        lax.fori_loop(atmos // 3, atmos, one, 0)

    @pl.when(is_atmos)
    def _():
        list_blocks()
        for place in range(ocean):
            fill(atmos, place)
        pl.semaphore_wait(
            barrier, 2 + has_lower.astype(jnp.int32) + has_upper.astype(jnp.int32)
        )

    def pack_x(step, chunk, source):
        for var in range(2):
            start = (var * levels + chunk * CHUNK) * 8
            here = pl.ds(pl.multiple_of(chunk * CHUNK, 8), CHUNK)
            x_out[step, 1, var, here, :] = source[pl.ds(start, CHUNK, stride=8), :]
            x_out[step, 0, var, here, :] = source[pl.ds(start + 7, CHUNK, stride=8), :]

    def add_lanes(low, high, value, entry):
        turned = pltpu.roll(value, 2 * entry, 1) if entry else value
        low = jnp.where(lane == 2 * entry, turned, low)
        high = jnp.where(lane == (2 * entry + 127) % 128, turned, high)
        return low, high

    def put_y(target, wall, low, high):
        target[1] = low
        target[0] = high

        @pl.when(no_lower)
        def _():
            wall[0] = pltpu.roll(low, 127, 1)

        @pl.when(no_upper)
        def _():
            wall[1] = pltpu.roll(high, 1, 1)

    def copy_x(step, chunk, side):
        here = pl.ds(pl.multiple_of(chunk * CHUNK, 8), CHUNK)
        return pltpu.make_async_remote_copy(
            src_ref=x_out.at[step, side, :, here, :],
            dst_ref=x_in.at[step, side, :, here, :],
            send_sem=x_send.at[step, side, chunk],
            recv_sem=x_recv.at[step, side, chunk],
            device_id=(row, left if side else right),
            device_id_type=MESH,
        )

    def copy_y(step, chunk, side):
        return pltpu.make_async_remote_copy(
            src_ref=y_out.at[step, chunk, side],
            dst_ref=y_in.at[step, chunk, side],
            send_sem=y_send.at[step, side, chunk],
            recv_sem=y_recv.at[step, side, chunk],
            device_id=(row - 1 if side else row + 1, tile),
            device_id_type=MESH,
        )

    def copy_x0(side):
        return pltpu.make_async_remote_copy(
            src_ref=x0_out.at[side],
            dst_ref=x0_in.at[side],
            send_sem=x0_send.at[side],
            recv_sem=x0_recv.at[side],
            device_id=(row, left if side else right),
            device_id_type=MESH,
        )

    def copy_y0(side):
        return pltpu.make_async_remote_copy(
            src_ref=y0_out.at[side],
            dst_ref=y0_in.at[side],
            send_sem=y0_send.at[side],
            recv_sem=y0_recv.at[side],
            device_id=(row - 1 if side else row + 1, tile),
            device_id_type=MESH,
        )

    def start_edges(step, chunk):
        copy_x(step, chunk, 0).start()
        copy_x(step, chunk, 1).start()

        @pl.when(has_lower)
        def _():
            copy_y(step, chunk, 1).start()

        @pl.when(has_upper)
        def _():
            copy_y(step, chunk, 0).start()

    def await_edges(step, chunk):
        copy_x(step, chunk, 0).wait_recv()
        copy_x(step, chunk, 1).wait_recv()

        @pl.when(has_lower)
        def _():
            copy_y(step, chunk, 0).wait_recv()

        @pl.when(has_upper)
        def _():
            copy_y(step, chunk, 1).wait_recv()

    def end_edges(step, chunk):
        copy_x(step, chunk, 0).wait_send()
        copy_x(step, chunk, 1).wait_send()

        @pl.when(has_lower)
        def _():
            copy_y(step, chunk, 1).wait_send()

        @pl.when(has_upper)
        def _():
            copy_y(step, chunk, 0).wait_send()

    get_tracers.wait()

    def pack_first(turn, carry):
        chunk = chunks - 1 - turn
        pack_x(0, chunk, first)
        low = high = jnp.zeros((8, 128), jnp.float32)
        for level in range(CHUNK):
            for var in range(2):
                value = first[tile_of(var * levels + chunk * CHUNK + level), :]
                low, high = add_lanes(low, high, value, 2 * level + var)
        put_y(y_out.at[0, chunk], y_in.at[0, chunk], low, high)
        return carry

    lax.fori_loop(0, chunks, pack_first, 0)

    def await_blocks(place):
        pltpu.make_async_copy(
            incoming.at[place], incoming.at[place], remap_recv.at[place]
        ).wait()

    @pl.when(is_ocean)
    def _():
        releases = (
            first_of_left.astype(jnp.int32)
            + first_of_right.astype(jnp.int32)
            + has_upper.astype(jnp.int32)
            + middle.astype(jnp.int32)
        )

        @pl.when(releases > 0)
        def _():
            pl.semaphore_wait(go, releases)

    def send_first(turn, carry):
        start_edges(0, chunks - 1 - turn)
        return carry

    lax.fori_loop(0, chunks, send_first, 0)

    get_vertical.wait()
    get_lateral.wait()
    rate[0] = jnp.zeros((8, 128), jnp.float32)
    rate[levels] = jnp.zeros((8, 128), jnp.float32)

    def one_rate(level, carry):
        value = ver[level].astype(jnp.float32)
        rate[level + 1] = jnp.where(level + 1 < live_levels, value, 0.0)
        return carry

    lax.fori_loop(0, levels - 1, one_rate, 0, unroll=8)

    def sides_of(value, x_low, x_high, merged, entry):
        ends = pltpu.roll(merged, 127 - 2 * entry, 1)
        return (
            jnp.where(sub == 0, x_low, pltpu.roll(value, 1, 0))
            + jnp.where(sub == 7, x_high, pltpu.roll(value, 7, 0))
        ) + (
            jnp.where(lane == 0, ends, pltpu.roll(value, 1, 1))
            + jnp.where(lane == 127, ends, pltpu.roll(value, 127, 1))
        )

    def advance(step, chunk, source, target, merged, edges):
        lateral_here = lat[...].astype(jnp.float32)
        base = chunk * CHUNK
        previous = [None, None]
        centre = [None, None]
        low = high = jnp.zeros((8, 128), jnp.float32)
        for var in range(2):
            centre[var] = source[tile_of(var * levels + base), :]
            above = source[tile_of(var * levels + jnp.maximum(base - 1, 0)), :]
            previous[var] = rate[base] * (centre[var] - above)
        for level in range(CHUNK):
            here = base + level
            mixing = rate[here + 1]
            spreading = jnp.where(here < live_levels, lateral_here, 0.0)
            for var in range(2):
                entry = 2 * level + var
                after = jnp.minimum(here + 1, levels - 1) if level == CHUNK - 1 else here + 1
                value = centre[var]
                below = source[tile_of(var * levels + after), :]
                x_low = jnp.broadcast_to(x_in[step, 0, var, pl.ds(here, 1), :], (8, 128))
                x_high = jnp.broadcast_to(x_in[step, 1, var, pl.ds(here, 1), :], (8, 128))
                sides = sides_of(value, x_low, x_high, merged, entry)
                down = mixing * (below - value)
                result = value + spreading * (sides - 4.0 * value) + (down - previous[var])
                target[tile_of(var * levels + here), :] = result
                if edges:
                    low, high = add_lanes(low, high, result, entry)
                centre[var] = below
                previous[var] = down
        return low, high

    def merge(low, high):
        return jnp.where(lane % 2 == 1, pltpu.roll(low, 2, 1), high)

    def step_one(turn, carry):
        chunk = chunks - 1 - turn
        await_edges(0, chunk)
        merged = merge(y_in[0, chunk, 0], y_in[0, chunk, 1])
        low, high = advance(0, chunk, first, second, merged, True)
        pack_x(1, chunk, second)
        put_y(y_out.at[1, chunk], y_in.at[1, chunk], low, high)
        start_edges(1, chunk)
        return carry


    get_recvs.wait()
    get_gain.wait()

    def place_blocks(base, place):
        await_blocks(place)
        for slot in range(2):
            lands = sub == recvs[slot, base + place]
            column = pl.ds(pl.multiple_of((place * 2 + slot) * 128, 128), 128)
            for pair in range(2):
                value = jnp.concatenate(
                    [
                        jnp.where(
                            lands,
                            jnp.broadcast_to(
                                incoming[place, slot * 4 + field : slot * 4 + field + 1, :],
                                (8, 128),
                            ),
                            0.0,
                        )
                        for field in (2 * pair, 2 * pair + 1)
                    ],
                    axis=0,
                )
                coarse = value.astype(jnp.bfloat16)
                fine = (value - coarse.astype(jnp.float32)).astype(jnp.bfloat16)
                spread[16 * pair : 16 * pair + 16, column] = coarse
                spread[32 + 16 * pair : 48 + 16 * pair, column] = fine

    def product(start, count):
        return jnp.dot(
            spread[:, start * 256 : (start + count) * 256],
            wts[start : start + count].reshape(count * 256, 128),
            preferred_element_type=jnp.float32,
        )

    def force(total):
        remapped = total[:32] + total[32:]
        values = []
        for var in range(2):
            value = gains[var, 0] * remapped[:8]
            for field in range(1, 4):
                value = value + gains[var, field] * remapped[8 * field : 8 * field + 8]
            forcing[var] = value
            values.append(value)
        x0_out[0] = jnp.where(sub == 0, values[0][7:8, :], values[1][7:8, :])
        x0_out[1] = jnp.where(sub == 0, values[0][0:1, :], values[1][0:1, :])
        copy_x0(0).start()
        copy_x0(1).start()
        low = high = jnp.zeros((8, 128), jnp.float32)
        for var in range(2):
            low, high = add_lanes(low, high, values[var], var)
        put_y(y0_out, y0_in, low, high)

        @pl.when(has_lower)
        def _():
            copy_y0(1).start()

        @pl.when(has_upper)
        def _():
            copy_y0(0).start()

    def exchange():
        @pl.when(is_atmos)
        def _():
            get_weights(atmos, ocean).wait()
            total = jnp.zeros((64, 128), jnp.float32)
            part = max(ocean // 4, 1)
            for start in range(0, ocean, part):
                for place in range(start, start + part):
                    place_blocks(atmos, place)
                total = total + product(start, part)
            force(total)
            for place in range(ocean):
                send_block(atmos, place, 0)

            @pl.when(helps)
            def _():
                pl.semaphore_wait(here, ocean // share)
                for turn in range(ocean // share):
                    pl.semaphore_signal(
                        go,
                        inc=1,
                        device_id=(atmos + turn * share + row, tile),
                        device_id_type=MESH,
                    )

        @pl.when(is_ocean)
        def _():
            def one(place, carry):
                place_blocks(0, place)
                return carry

            lax.fori_loop(0, atmos, one, 0)
            get_weights(0, atmos).wait()
            force(product(0, atmos))

    forced_first = jnp.logical_and(row >= 2 * atmos // 3, is_atmos)
    steps_first = jnp.where(forced_first, 1, 0)

    def phase(turn, carry):
        @pl.when(turn == steps_first)
        def _():
            lax.fori_loop(0, chunks, step_one, 0)

        @pl.when(turn != steps_first)
        def _():
            exchange()

        return carry

    lax.fori_loop(0, 2, phase, 0)

    def step_two(turn, carry):
        chunk = chunks - 1 - turn
        await_edges(1, chunk)
        merged = merge(y_in[1, chunk, 0], y_in[1, chunk, 1])
        advance(1, chunk, second, out, merged, False)
        return carry

    lax.fori_loop(0, chunks, step_two, 0)
    for step in range(2):

        def end(chunk, carry):
            end_edges(step, chunk)
            return carry

        lax.fori_loop(0, chunks, end, 0)

    lateral_here = lat[...].astype(jnp.float32)
    for var in range(2):
        value = forcing[var]
        mixing = rate[1] * value
        out[tile_of(var * levels), :] += 2.0 * value - mixing - 4.0 * lateral_here * value
        out[tile_of(var * levels + 1), :] += mixing

    copy_x0(0).wait_send()
    copy_x0(1).wait_send()

    @pl.when(has_lower)
    def _():
        copy_y0(1).wait_send()
        copy_y0(0).wait_recv()

    @pl.when(has_upper)
    def _():
        copy_y0(0).wait_send()
        copy_y0(1).wait_recv()

    @pl.when(is_ocean)
    def _():
        pltpu.make_async_copy(
            outgoing.at[pl.ds(0, atmos)], outgoing.at[pl.ds(0, atmos)], remap_send
        ).wait()

    @pl.when(is_atmos)
    def _():
        pltpu.make_async_copy(
            outgoing.at[pl.ds(0, ocean)], outgoing.at[pl.ds(0, ocean)], remap_send
        ).wait()

    merged = merge(y0_in[0], y0_in[1])
    copy_x0(0).wait_recv()
    copy_x0(1).wait_recv()
    for var in range(2):
        x_low = jnp.broadcast_to(x0_in[0, var : var + 1, :], (8, 128))
        x_high = jnp.broadcast_to(x0_in[1, var : var + 1, :], (8, 128))
        out[tile_of(var * levels), :] += lateral_here * sides_of(
            forcing[var], x_low, x_high, merged, var
        )


def per_device(
    tracers,
    surface_fields,
    lateral_rate,
    vertical_rate,
    coupling_gain,
    send_slots,
    recv_slots,
    remap_weights,
):
    rows = lax.axis_size("comp")
    atmos = 3 * rows // 4
    levels = tracers.shape[1]
    chunks = levels // CHUNK
    cells = 2 * levels * 8
    f32, bf16, i32 = jnp.float32, jnp.bfloat16, jnp.int32
    hbm = pl.BlockSpec(memory_space=pltpu.HBM)
    dma = pltpu.SemaphoreType.DMA
    result = pl.pallas_call(
        functools.partial(kernel, levels),
        out_shape=pltpu.VMEM((cells, 128), f32),
        in_specs=[hbm] * 8,
        out_specs=pl.BlockSpec(memory_space=pltpu.VMEM),
        scratch_shapes=[
            pltpu.VMEM((cells + 8, 128), f32),
            pltpu.VMEM((cells + 8, 128), f32),
            pltpu.VMEM((8, 128), bf16),
            pltpu.VMEM((levels - 1, 8, 128), bf16),
            pltpu.VMEM((levels + 1, 8, 128), f32),
            pltpu.VMEM((40, 128), f32),
            pltpu.VMEM((9, 8, 128), f32),
            pltpu.VMEM((atmos, 8, 128), f32),
            pltpu.VMEM((atmos, 8, 128), f32),
            pltpu.VMEM((64, atmos * 256), bf16),
            pltpu.VMEM((atmos, 256, 128), bf16),
            pltpu.VMEM((2, 8, 128), f32),
            pltpu.SMEM((2, 4), f32),
            pltpu.SMEM((2, rows), i32),
            pltpu.SMEM((2, rows), i32),
            pltpu.VMEM((2, 2, 2, levels, 128), f32),
            pltpu.VMEM((2, 2, 2, levels, 128), f32),
            pltpu.VMEM((2, chunks, 2, 8, 128), f32),
            pltpu.VMEM((2, chunks, 2, 8, 128), f32),
            pltpu.VMEM((2, 8, 128), f32),
            pltpu.VMEM((2, 8, 128), f32),
            pltpu.VMEM((2, 8, 128), f32),
            pltpu.VMEM((2, 8, 128), f32),
            dma((8,)),
            dma,
            dma((atmos,)),
            dma((2, 2, chunks)),
            dma((2, 2, chunks)),
            dma((2, 2, chunks)),
            dma((2, 2, chunks)),
            dma((2,)),
            dma((2,)),
            dma((2,)),
            dma((2,)),
            pltpu.SemaphoreType.REGULAR,
            pltpu.SemaphoreType.REGULAR,
        ],
        compiler_params=pltpu.CompilerParams(
            collective_id=0, has_side_effects=True, vmem_limit_bytes=48 * 1024 * 1024
        ),
        cost_estimate=pl.CostEstimate(
            flops=60_000_000, bytes_accessed=4_000_000, transcendentals=0
        ),
    )(
        *[
            pltpu.with_memory_space_constraint(array, pltpu.HBM)
            for array in (
                tracers.reshape(cells, 128),
                surface_fields.reshape(32, 128),
                lateral_rate,
                vertical_rate,
                coupling_gain[0],
                jnp.transpose(send_slots[0, :, 0]),
                jnp.transpose(recv_slots[0, :, 0]),
                remap_weights.reshape(rows, 256, 128),
            )
        ]
    )
    return result.reshape(tracers.shape)


def solution(mesh):
    return jax.shard_map(
        per_device,
        mesh=mesh,
        in_specs=(
            P(None, None, "tile", "comp"),
            P(None, "tile", "comp"),
            P("tile", "comp"),
            P(None, "tile", "comp"),
            P("comp", None, None),
            P("comp", None, "tile", None),
            P("comp", None, "tile", None),
            P("comp", None, "tile", None, None, None),
        ),
        out_specs=P(None, None, "tile", "comp"),
        check_vma=False,
    )
```
